512 devices in a mesh: corpus: 64 (over z, y_lo, core), tensor: 8 (over y_hi, x).
Axes of the slice: x: 4, y: 8 (y_hi: 2, y_lo: 4; y = y_hi * 4 + y_lo), z: 8, core: 2. Of those that a mesh axis runs over, the one named last changes fastest.
Arguments:
- query_rows: bfloat16 [64, 8, 4096], P('corpus', None, 'tensor'), may hold values from -6 to 6
- corpus_rows: bfloat16 [512, 24, 4096], P('corpus', None, 'tensor'), may hold values from -6 to 6
- passage_length: int32 [512], replicated, may hold values from 1 to 24, 6144 in all
- candidate_owner: int32 [64, 8], P('corpus'), may hold values from 0 to 63, all different within a row
- candidate_slot: int32 [64, 8], P('corpus'), may hold values from 0 to 7
- norm_gain: bfloat16 [4096], P('tensor'), may hold values from 0.099609375 to 1.8984375
- project_weight: bfloat16 [4096, 3, 2048], P('corpus', None, 'tensor'), may hold values from -3 to 3
- output_weight: bfloat16 [2048, 4096], P('tensor', 'corpus'), may hold values from -0.375 to 0.375
Outputs:
- layer_output: bfloat16 [16384, 4096], P('corpus', 'tensor')
The draws below stay inside these ranges and needn't reach their ends.
Inputs may be any that keep to these rules, and one draw needn't show every extreme that they name: `candidate_owner`: the 8 candidates of a group lie on 8 different owner shards.
All inputs are finite; a program needn't handle non-finite values.
Results may differ from the reference program's by a relative error of at most 0.018.
The reference program's roundings to bfloat16 on the way count: a program that leaves them out, or rounds other values in their place, can miss the bound.
Values may be sent and summed in bfloat16 or wider, within the bound.
No kernel may reach another device: no remote copies, remote signals or barrier semaphores. Data moves between devices by JAX's collectives and lax.ppermute only.
A program may use at most 64 MiB of HBM per device.

```python
import math
import jax
import jax.numpy as jnp
import numpy as np
from jax import lax

D = 4096
HEADS = 16
HEAD_DIM = 128
QLEN = 8
PLEN = 24
SEQ = 32
PAIRS = 8
PASS_DEV = 8
GROUPS = 64
PASSAGES = 512
N_TENSOR = 8


def draw_project_weight(key, part):
    key = jax.random.fold_in(key, 7)
    base = jnp.clip(jax.random.normal(key, (D, 3, HEADS * HEAD_DIM), jnp.float32), -4.0, 4.0) / jnp.sqrt(jnp.float32(D))
    return base.astype(jnp.bfloat16)


def place_ends(entries, rng, least, top_value):
    longest = entries.shape.index(max(entries.shape))
    spots = []
    for shift in (0, 1):
        where = [jax.random.randint(jax.random.fold_in(rng, axis), (), 0, length) for axis, length in enumerate(entries.shape)]
        where[longest] = (where[longest] + shift) % entries.shape[longest]
        spots.append(tuple(where))
    return entries.at[spots[0]].set(least).at[spots[1]].set(top_value)


def levels(key, dims, pieces, low, largest):
    factor_of = 1.0
    for axis_at, blocks in pieces:
        heights = jax.random.uniform(jax.random.fold_in(jax.random.fold_in(key, 6), axis_at), (blocks,), jnp.float32, low / len(pieces), largest / len(pieces))
        factor_of = factor_of * jnp.repeat(jnp.exp(heights), dims[axis_at] // blocks).reshape((-1,) + (1,) * (len(dims) - 1 - axis_at))
    return factor_of


def distinct(key, rows, count, top, lift):
    ranking = jax.random.permutation(jax.random.fold_in(key, 1), count)
    boost = ranking
    for power in range(3):
        boost = boost * boost // count
    boost = boost * lift // count
    tickets = jax.random.randint(jax.random.fold_in(key, 2), (rows, count), 0, 4096) + boost
    sure = jax.random.permutation(jax.random.fold_in(key, 3), rows)[jnp.arange(count) % rows]
    tickets = jnp.where(jnp.arange(rows)[:, None] == sure[None, :], 1 << 14, tickets)
    priority = tickets * count + jnp.arange(count)
    return lax.top_k(priority.astype(jnp.int32), top)[1].astype(jnp.int32)


def profile(number_of, total, limit, lean):
    weights = [(1 << 20) // math.isqrt(standing ** lean) + 1 for standing in range(2, number_of + 1)]
    rest, holding = total - limit - (number_of - 1), [1] * (number_of - 1)
    while rest > 0:
        candidates = [i for i in range(number_of - 1) if holding[i] < limit]
        whole, left = sum([weights[i] for i in candidates]), rest
        for i in candidates:
            addition = min(limit - holding[i], max(1, left * weights[i] // whole), rest)
            holding[i] = holding[i] + addition
            rest = rest - addition
    return np.array([limit] + holding)


def ragged(rng, number_of, total, most, lean):
    if number_of == 2:
        one = jax.random.randint(rng, (), max(1, total - most), min(most, total - 1) + 1)
        return jnp.stack([one, total - one])
    lengths = jnp.asarray(profile(number_of, total, most, lean), jnp.int32)
    twos = (number_of - 1) // 2
    source_of, taker = lengths[1:1 + 2 * twos:2], lengths[2:2 + 2 * twos:2]
    margin = jnp.minimum(source_of - 1, most - taker)
    passed = jax.random.randint(jax.random.fold_in(rng, 1), (twos,), 0, 1 << 20) % (margin + 1)
    lengths = lengths.at[1:1 + 2 * twos:2].set(source_of - passed).at[2:2 + 2 * twos:2].set(taker + passed)
    return lengths[jax.random.permutation(jax.random.fold_in(rng, 2), number_of)]


def gaussian(rng, extent, deviation, limit, split=(), kind=jnp.bfloat16):
    result = jax.random.normal(rng, extent, jnp.float32) * deviation
    if len(split) > 0:
        result = levels(rng, extent, split, -0.22, 0.18) * result
    return jnp.clip(result, min=-limit, max=limit).astype(kind)


def setup_inputs(seed: int = 0) -> dict:
    splits = jax.random.split(jax.random.key(seed), 9)
    return {
        "query_rows": gaussian(splits[0], (GROUPS, QLEN, D), 1.0, 6.0, ((0, 64), (2, 8))),
        "corpus_rows": gaussian(splits[1], (PASSAGES, PLEN, D), 1.0, 6.0, ((0, 64), (2, 8))),
        "passage_length": ragged(splits[2], PASSAGES, PASSAGES * PLEN // 2, PLEN, 2).astype(jnp.int32),
        "candidate_owner": distinct(splits[3], GROUPS, GROUPS, PAIRS, 2048),
        "candidate_slot": place_ends(jax.random.randint(splits[4], (GROUPS, PAIRS), 0, PASS_DEV), jax.random.fold_in(splits[4], 1), 0, PASS_DEV - 1).astype(jnp.int32),
        "norm_gain": jnp.clip(1.0 + 0.18 * jax.random.normal(splits[5], (D,), jnp.float32), 0.099609375, 1.8984375).astype(jnp.bfloat16),
        "project_weight": draw_project_weight(jax.random.fold_in(splits[8], 71), 0),
        "output_weight": gaussian(splits[7], (HEADS * HEAD_DIM, D), (2 * HEAD_DIM) ** -0.5, 0.375, ((0, 8), (1, 64))),
    }


def rotate_pairs(inputs, seq_len):
    half_size = inputs.shape[-1] // 2
    frequency = jnp.power(10000.0, -2.0 * jnp.arange(half_size, dtype=jnp.float32) / inputs.shape[-1])
    position = (jnp.arange(inputs.shape[0], dtype=jnp.int32) % seq_len).astype(jnp.float32)
    angles = position[:, None] * frequency[None, :]
    cosine_table = jnp.cos(angles)[:, None, :]
    sine_table = jnp.sin(angles)[:, None, :]
    first_part = inputs[..., :half_size]
    second_part = inputs[..., half_size:]
    return jnp.concatenate([first_part * cosine_table - second_part * sine_table, second_part * cosine_table + first_part * sine_table], axis=-1)

def attend(queries, keys, values, pair_count, seq_len, query_len):
    pair_total = pair_count.shape[0]
    head_count = queries.shape[1]
    head_dim = queries.shape[2]
    shape_four = (pair_total, seq_len, head_count, head_dim)
    scores = jnp.einsum('pqhd,pkhd->phqk', queries.reshape(shape_four).astype(jnp.float32), keys.reshape(shape_four).astype(jnp.float32)) * (1.0 / math_sqrt(head_dim))
    slots = jnp.arange(seq_len, dtype=jnp.int32)
    allowed = (slots[None, :] <= slots[:, None])[None, None] & (slots[None, None, None, :] < query_len + pair_count[:, None, None, None])
    scores = jnp.where(allowed, scores, -1e+30)
    row_max = lax.optimization_barrier(jnp.max(scores, axis=-1, keepdims=True))
    exponent = jnp.exp(scores - row_max)
    row_total = lax.optimization_barrier(jnp.sum(exponent, axis=-1, keepdims=True))
    attention_weights = (exponent / row_total).astype(jnp.bfloat16)
    attended = jnp.einsum('phqk,pkhd->pqhd', attention_weights.astype(jnp.float32), values.reshape(shape_four).astype(jnp.float32))
    return attended.astype(jnp.bfloat16).reshape(pair_total * seq_len, head_count * head_dim)

def math_sqrt(number):
    return float(number) ** 0.5

def reference(query_rows, corpus_rows, passage_length, candidate_owner, candidate_slot, norm_gain, project_weight, output_weight):
    row_count = PAIRS * SEQ
    per_device = HEADS * HEAD_DIM // N_TENSOR

    def one_group(items):
        query_block, owner_ids, slot_ids = items
        passage_index = (owner_ids * PASS_DEV + slot_ids).astype(jnp.int32)
        passages = jnp.take(corpus_rows, passage_index, axis=0)
        counts = jnp.take(passage_length, passage_index, axis=0)
        live_rows = jnp.arange(PLEN, dtype=jnp.int32)[None, :] < counts[:, None]
        passages = jnp.where(live_rows[:, :, None], passages, jnp.zeros((), passages.dtype))
        query_copy = jnp.broadcast_to(query_block[None], (PAIRS, QLEN, D))
        packed = jnp.concatenate([query_copy, passages], axis=1).reshape(row_count, D)
        widened = packed.astype(jnp.float32)
        inverse_rms = lax.rsqrt(lax.optimization_barrier(jnp.mean(widened * widened, axis=1, keepdims=True)) + 1e-05)
        normed = (widened * inverse_rms * norm_gain.astype(jnp.float32)[None, :]).astype(jnp.bfloat16)
        projected = jnp.dot(normed, project_weight.reshape(D, 3 * HEADS * HEAD_DIM), preferred_element_type=jnp.float32)
        projected = projected.reshape(row_count, 3, HEADS, HEAD_DIM)
        queries = rotate_pairs(projected[:, 0], SEQ).astype(jnp.bfloat16)
        keys = rotate_pairs(projected[:, 1], SEQ).astype(jnp.bfloat16)
        values = projected[:, 2].astype(jnp.bfloat16)
        attended = attend(queries, keys, values, counts, SEQ, QLEN)
        partial_value = jnp.einsum('rtn,tnd->rtd', attended.reshape(row_count, N_TENSOR, per_device).astype(jnp.float32), output_weight.reshape(N_TENSOR, per_device, D).astype(jnp.float32))
        partial_value = partial_value.astype(jnp.bfloat16)
        summed = lax.optimization_barrier(jnp.sum(partial_value.astype(jnp.float32), axis=1))
        return (widened + summed).astype(jnp.bfloat16)
    outputs = lax.map(one_group, (query_rows, candidate_owner, candidate_slot))
    return outputs.reshape(GROUPS * row_count, D)
```

```python
import jax
import jax.numpy as jnp
from jax import lax
from jax.sharding import Mesh, PartitionSpec as P

HEAD_DIM = 128
SPLIT = (("z", 8), ("y", 4), ("c", 2), ("h", 2), ("x", 4))
AXES = tuple(name for name, _ in SPLIT)
CORPUS = ("z", "y", "c")
TENSOR = ("h", "x")


def rotation_tables(position):
    half = HEAD_DIM // 2
    frequency = jnp.power(10000.0, -2.0 * jnp.arange(half, dtype=jnp.float32) / HEAD_DIM)
    angles = position.astype(jnp.float32)[:, None] * frequency[None, :]
    return jnp.cos(angles), jnp.sin(angles)


def rotate(inputs, cosine, sine):
    half = HEAD_DIM // 2
    first, second = inputs[:, :half], inputs[:, half:]
    return jnp.concatenate(
        [first * cosine - second * sine, second * cosine + first * sine], axis=-1
    ).astype(jnp.bfloat16)


def on_device(
    query_rows,
    corpus_rows,
    passage_length,
    candidate_owner,
    candidate_slot,
    norm_gain,
    project_weight,
    output_weight,
):
    bf16, f32, i32 = jnp.bfloat16, jnp.float32, jnp.int32
    sizes = dict(SPLIT)
    shards = sizes["z"] * sizes["y"] * sizes["c"]
    plane = sizes["y"] * sizes["c"]
    tensors = sizes["h"] * sizes["x"]
    core = lax.axis_index("c")
    stored, passage_rows, features = corpus_rows.shape
    query_len = query_rows.shape[1]
    pairs = candidate_owner.shape[1]
    rows = query_len + pairs * passage_rows
    depth = project_weight.shape[0]

    own_owner, own_slot = candidate_owner[0], candidate_slot[0]
    asks = jnp.arange(shards, dtype=i32)[:, None] == own_owner[None, :]
    request = jnp.sum(jnp.where(asks, own_slot[None, :] + 1, 0), axis=1)
    request = jnp.broadcast_to(request[:, None], (shards, 128))
    asked = lax.all_to_all(request, CORPUS, split_axis=0, concat_axis=0, tiled=True)
    wanted = jnp.clip(asked[:, 0] - 1, 0, stored - 1)

    wide = project_weight.reshape(depth, 3, 2, HEAD_DIM).transpose(2, 0, 1, 3)
    wide = wide.reshape(2, depth, 3 * HEAD_DIM)
    wide = jnp.broadcast_to(wide[None], (sizes["y"], 2, depth, 3 * HEAD_DIM))
    wide = wide.reshape(plane, depth, 3 * HEAD_DIM)
    wide = lax.all_to_all(wide, ("y", "c"), split_axis=0, concat_axis=0, tiled=True)
    wide = wide.reshape(plane * depth, 3 * HEAD_DIM)
    wide_own = lax.all_gather(wide, "z", axis=0, tiled=True)
    swap_core = [(0, 1), (1, 0)]
    wide_other = lax.ppermute(wide_own, "c", swap_core)

    cells = [(z, q, t) for z in range(sizes["z"]) for q in range(plane) for t in range(tensors)]
    number = {cell: i for i, cell in enumerate(cells)}
    turn = [(number[(z, q, t)], number[(t, q, z)]) for z, q, t in cells]
    narrow = lax.ppermute(output_weight.T, AXES, turn)
    narrow = narrow.reshape(depth, 2, HEAD_DIM).transpose(1, 0, 2)
    narrow = jnp.broadcast_to(narrow[None], (sizes["y"], 2, depth, HEAD_DIM))
    narrow = narrow.reshape(plane, depth, HEAD_DIM)
    narrow = lax.all_to_all(narrow, ("y", "c"), split_axis=0, concat_axis=0, tiled=True)
    narrow = narrow.reshape(1, plane * depth, HEAD_DIM)
    narrow_own = lax.all_gather(narrow, "z", axis=0, tiled=True)
    narrow_other = lax.ppermute(narrow_own, "c", swap_core)

    outgoing = jnp.take(corpus_rows, wanted, axis=0, mode="clip")
    arrived = lax.all_to_all(outgoing, CORPUS, split_axis=0, concat_axis=0, tiled=True)
    counts = jnp.take(passage_length, own_owner * stored + own_slot, axis=0, mode="clip")
    passages = jnp.take(arrived, own_owner, axis=0, mode="clip")
    inside = jnp.arange(passage_rows, dtype=i32)[None, :] < counts[:, None]
    passages = jnp.where(inside[:, :, None], passages, jnp.zeros((), bf16))
    packed = jnp.concatenate([query_rows[0], passages.reshape(-1, features)], axis=0)

    far = lax.ppermute(packed, "h", [(0, 1), (1, 0)])
    low = lax.axis_index("h") == 0
    both = jnp.stack([jnp.where(low, packed, far), jnp.where(low, far, packed)])
    spread = jnp.broadcast_to(both[None], (sizes["x"],) + both.shape)
    full = lax.all_to_all(spread, "x", split_axis=0, concat_axis=0, tiled=True)
    full = full.transpose(2, 1, 0, 3).reshape(rows, tensors * features)
    gain = lax.all_gather(norm_gain, TENSOR, axis=0, tiled=True)
    widened = full.astype(f32)
    mean = jnp.mean(widened * widened, axis=1, keepdims=True)
    normed = (widened * lax.rsqrt(mean + 1e-05) * gain.astype(f32)[None, :]).astype(bf16)

    row = jnp.arange(rows, dtype=i32)
    is_query = row < query_len
    place = (row - query_len) % passage_rows
    slot = jnp.where(is_query, row, query_len + place)
    pair = jnp.where(is_query, -1, (row - query_len) // passage_rows)
    count_of = jnp.concatenate(
        [jnp.full((query_len,), passage_rows, i32), jnp.repeat(counts, passage_rows)]
    )
    allowed = (slot[None, :] <= slot[:, None]) & (
        is_query[None, :]
        | ((pair[None, :] == pair[:, None]) & (slot < query_len + count_of)[None, :])
    )
    cosine, sine = rotation_tables(slot)

    def head(weight):
        projected = jnp.dot(normed, weight, preferred_element_type=f32)
        queries = rotate(projected[:, :HEAD_DIM], cosine, sine)
        keys = rotate(projected[:, HEAD_DIM : 2 * HEAD_DIM], cosine, sine)
        values = projected[:, 2 * HEAD_DIM :].astype(bf16)
        scores = lax.dot_general(
            queries, keys, (((1,), (1,)), ((), ())), preferred_element_type=f32
        ) * (1.0 / float(HEAD_DIM) ** 0.5)
        scores = jnp.where(allowed, scores, -1e30)
        exponent = jnp.exp(scores - jnp.max(scores, axis=-1, keepdims=True))
        weights = (exponent / jnp.sum(exponent, axis=-1, keepdims=True)).astype(bf16)
        return jnp.dot(weights, values, preferred_element_type=f32).astype(bf16)

    mine, theirs = head(wide_own), head(wide_other)
    first = core == 0
    attended = jnp.concatenate(
        [jnp.where(first, mine, theirs), jnp.where(first, theirs, mine)], axis=1
    )
    spread = jnp.broadcast_to(attended[None], (tensors,) + attended.shape)
    heads = lax.all_to_all(spread, TENSOR, split_axis=0, concat_axis=0, tiled=True)
    low_head, high_head = heads[:, :, :HEAD_DIM], heads[:, :, HEAD_DIM:]
    near_head = jnp.where(first, low_head, high_head)
    far_head = jnp.where(first, high_head, low_head)
    numbers = (((2,), (2,)), ((0,), (0,)))
    partial_value = lax.dot_general(
        near_head, narrow_own, numbers, preferred_element_type=f32
    ) + lax.dot_general(far_head, narrow_other, numbers, preferred_element_type=f32)
    summed = jnp.sum(partial_value.astype(bf16).astype(f32), axis=0)
    final = (packed.astype(f32) + summed).astype(bf16)
    query_out = jnp.broadcast_to(final[None, :query_len], (pairs, query_len, features))
    passage_out = final[query_len:].reshape(pairs, passage_rows, features)
    return jnp.concatenate([query_out, passage_out], axis=1).reshape(-1, features)


def solution(mesh):
    fine = Mesh(mesh.devices.reshape([size for _, size in SPLIT]), AXES)
    placed = (
        P(CORPUS, None, TENSOR),
        P(CORPUS, None, TENSOR),
        P(),
        P(CORPUS, None),
        P(CORPUS, None),
        P(TENSOR),
        P(CORPUS, None, TENSOR),
        P(TENSOR, CORPUS),
    )
    return jax.shard_map(
        on_device, mesh=fine, in_specs=placed, out_specs=P(CORPUS, TENSOR), check_vma=False
    )
```

```python
import functools

import jax
import jax.numpy as jnp
from jax import lax
from jax.experimental import pallas as pl
from jax.experimental.pallas import tpu as pltpu
from jax.sharding import Mesh, PartitionSpec as P

HEAD_DIM = 128
ROW_TILE = 16
SPLIT = (("z", 8), ("y", 4), ("c", 2), ("h", 2), ("x", 4))
SIZE = dict(SPLIT)
AXES = tuple(name for name, _ in SPLIT)
CORPUS = ("z", "y", "c")
TENSOR = ("h", "x")
SWAP = [(0, 1), (1, 0)]
VMEM = pl.BlockSpec(memory_space=pltpu.VMEM)


def attention_kernel(full_ref, own_ref, other_ref, cos_ref, sin_ref, mask_ref, out_ref, normed_ref, *, gain_row):
    bf16, f32 = jnp.bfloat16, jnp.float32
    spread, highs, rows, features = full_ref.shape
    width = spread * highs * features
    total = jnp.zeros((rows, HEAD_DIM), f32)
    for x in range(spread):
        for h in range(highs):
            chunk = full_ref[x, h].astype(f32)
            square = chunk * chunk
            for lane in range(0, features, HEAD_DIM):
                total = total + square[:, lane : lane + HEAD_DIM]
    inverse = lax.rsqrt(jnp.sum(total, axis=1, keepdims=True) / width + 1e-05)
    for x in range(spread):
        for h in range(highs):
            chunk = full_ref[x, h].astype(f32)
            gain = chunk[gain_row : gain_row + 1, :]
            begin = (h * spread + x) * features
            normed_ref[:, begin : begin + features] = (chunk * inverse * gain).astype(bf16)

    def rotate(inputs):
        return (
            inputs * cos_ref[...] + pltpu.roll(inputs, HEAD_DIM // 2, 1) * sin_ref[...]
        ).astype(bf16)

    def head(weight_ref):
        projected = jnp.dot(normed_ref[...], weight_ref[...], preferred_element_type=f32)
        queries = rotate(projected[:, :HEAD_DIM])
        keys = rotate(projected[:, HEAD_DIM : 2 * HEAD_DIM])
        values = projected[:, 2 * HEAD_DIM :].astype(bf16)
        scores = lax.dot_general(
            queries, keys, (((1,), (1,)), ((), ())), preferred_element_type=f32
        ) * (1.0 / float(HEAD_DIM) ** 0.5)
        scores = jnp.where(mask_ref[...] > 0, scores, -1e30)
        exponent = jnp.exp(scores - jnp.max(scores, axis=-1, keepdims=True))
        weights = (exponent / jnp.sum(exponent, axis=-1, keepdims=True)).astype(bf16)
        return jnp.dot(weights, values, preferred_element_type=f32).astype(bf16)

    mine, theirs = head(own_ref), head(other_ref)
    first = lax.axis_index("c") == 0
    out_ref[:, :HEAD_DIM] = jnp.where(first, mine, theirs)
    out_ref[:, HEAD_DIM:] = jnp.where(first, theirs, mine)


def output_kernel(heads_ref, own_ref, other_ref, packed_ref, out_ref, *, query_len, pairs, passage_rows):
    bf16, f32 = jnp.bfloat16, jnp.float32
    first = lax.axis_index("c") == 0
    numbers = (((1,), (1,)), ((), ()))
    summed = jnp.zeros(packed_ref.shape, f32)
    for t in range(heads_ref.shape[0]):
        low, high = heads_ref[t, :, :HEAD_DIM], heads_ref[t, :, HEAD_DIM:]
        near, far = jnp.where(first, low, high), jnp.where(first, high, low)
        partial_value = lax.dot_general(
            near, own_ref[t], numbers, preferred_element_type=f32
        ) + lax.dot_general(far, other_ref[t], numbers, preferred_element_type=f32)
        summed = summed + partial_value.astype(bf16).astype(f32)
    final = packed_ref[...].astype(f32) + summed
    blocks = []
    for pair in range(pairs):
        begin = query_len + pair * passage_rows
        blocks += [final[:query_len], final[begin : begin + passage_rows]]
    out_ref[...] = jnp.concatenate(blocks, axis=0).astype(bf16)


def shift(value, axis, step):
    count = SIZE[axis]
    return lax.ppermute(value, axis, [(i, (i + step) % count) for i in range(count)])


def gather_plane(blocks):
    first = lax.axis_index("c") == 0
    mine = jnp.where(first, blocks[0], blocks[1])
    got = lax.ppermute(jnp.where(first, blocks[1], blocks[0]), "c", SWAP)
    pair = jnp.concatenate([jnp.where(first, mine, got), jnp.where(first, got, mine)], axis=0)
    pieces = jnp.stack([pair] + [shift(pair, "y", step) for step in range(1, SIZE["y"])])
    order = (lax.axis_index("y") - jnp.arange(SIZE["y"], dtype=jnp.int32)) % SIZE["y"]
    pieces = jnp.take(pieces, order, axis=0, mode="clip")
    return pieces.reshape(-1, pieces.shape[2])


def on_device(
    query_rows,
    corpus_rows,
    passage_length,
    candidate_owner,
    candidate_slot,
    norm_gain,
    project_weight,
    output_weight,
):
    bf16, f32, i32 = jnp.bfloat16, jnp.float32, jnp.int32
    shards = SIZE["z"] * SIZE["y"] * SIZE["c"]
    plane = SIZE["y"] * SIZE["c"]
    tensors = SIZE["h"] * SIZE["x"]
    stored, passage_rows, features = corpus_rows.shape
    query_len = query_rows.shape[1]
    pairs = candidate_owner.shape[1]
    live = query_len + pairs * passage_rows
    rows = (live // ROW_TILE + 1) * ROW_TILE
    depth = project_weight.shape[0]

    wide = project_weight.reshape(depth, 3, 2, HEAD_DIM).transpose(2, 0, 1, 3)
    wide = gather_plane(wide.reshape(2, depth, 3 * HEAD_DIM))

    own_owner, own_slot = candidate_owner[0], candidate_slot[0]
    asks = jnp.arange(shards, dtype=i32)[:, None] == own_owner[None, :]
    request = jnp.sum(jnp.where(asks, own_slot[None, :] + 1, 0), axis=1)
    request = jnp.broadcast_to(request[:, None], (shards, 128))
    asked = lax.all_to_all(request, CORPUS, split_axis=0, concat_axis=0, tiled=True)
    wanted = jnp.clip(asked[:, 0] - 1, 0, stored - 1)

    wide_own = lax.all_gather(wide, "z", axis=0, tiled=True)
    wide_other = lax.ppermute(wide_own, "c", SWAP)
    cells = [(z, q, t) for z in range(SIZE["z"]) for q in range(plane) for t in range(tensors)]
    number = {cell: i for i, cell in enumerate(cells)}
    turn = [(number[(z, q, t)], number[(t, q, z)]) for z, q, t in cells]
    narrow = lax.ppermute(output_weight.T, AXES, turn)
    narrow, wanted = lax.optimization_barrier((narrow, wanted))
    narrow = gather_plane(narrow.reshape(depth, 2, HEAD_DIM).transpose(1, 0, 2))
    narrow_own = lax.all_gather(narrow[None], "z", axis=0, tiled=True)
    narrow_other = lax.ppermute(narrow_own, "c", SWAP)

    outgoing = jnp.take(corpus_rows, wanted, axis=0, mode="clip")
    arrived = lax.all_to_all(outgoing, CORPUS, split_axis=0, concat_axis=0, tiled=True)
    counts = jnp.take(passage_length, own_owner * stored + own_slot, axis=0, mode="clip")
    passages = jnp.take(arrived, own_owner, axis=0, mode="clip")
    inside = jnp.arange(passage_rows, dtype=i32)[None, :] < counts[:, None]
    passages = jnp.where(inside[:, :, None], passages, jnp.zeros((), bf16))
    packed = jnp.concatenate(
        [
            query_rows[0],
            passages.reshape(-1, features),
            norm_gain[None],
            jnp.zeros((rows - live - 1, features), bf16),
        ],
        axis=0,
    )

    far = lax.ppermute(packed, "h", SWAP)
    low = lax.axis_index("h") == 0
    both = jnp.stack([jnp.where(low, packed, far), jnp.where(low, far, packed)])
    spread = jnp.broadcast_to(both[None], (SIZE["x"],) + both.shape)
    full = lax.all_to_all(spread, "x", split_axis=0, concat_axis=0, tiled=True)

    row = jnp.arange(rows, dtype=i32)
    is_query = row < query_len
    slot = jnp.where(is_query, row, query_len + (row - query_len) % passage_rows)
    pair = jnp.where(is_query, -1, (row - query_len) // passage_rows)
    count_of = jnp.concatenate(
        [
            jnp.full((query_len,), passage_rows, i32),
            jnp.repeat(counts, passage_rows),
            jnp.zeros((rows - live,), i32),
        ]
    )
    allowed = (slot[None, :] <= slot[:, None]) & (
        is_query[None, :]
        | ((pair[None, :] == pair[:, None]) & (slot < query_len + count_of)[None, :])
    )
    half = HEAD_DIM // 2
    frequency = jnp.power(10000.0, -2.0 * jnp.arange(half, dtype=f32) / HEAD_DIM)
    angles = slot.astype(f32)[:, None] * frequency[None, :]
    cosine, sine = jnp.cos(angles), jnp.sin(angles)

    attended = pl.pallas_call(
        functools.partial(attention_kernel, gain_row=live),
        out_shape=jax.ShapeDtypeStruct((rows, 2 * HEAD_DIM), bf16),
        in_specs=[VMEM] * 6,
        out_specs=VMEM,
        scratch_shapes=[pltpu.VMEM((rows, tensors * features), bf16)],
        compiler_params=pltpu.CompilerParams(vmem_limit_bytes=32 * 1024 * 1024),
        cost_estimate=pl.CostEstimate(
            flops=2 * rows * tensors * features * 6 * HEAD_DIM,
            bytes_accessed=8 * 1024 * 1024,
            transcendentals=2 * rows * rows,
        ),
        name="attention",
    )(
        full,
        wide_own,
        wide_other,
        jnp.concatenate([cosine, cosine], axis=1),
        jnp.concatenate([-sine, sine], axis=1),
        allowed.astype(f32),
    )

    spread = jnp.broadcast_to(attended[None], (tensors,) + attended.shape)
    heads = lax.all_to_all(spread, TENSOR, split_axis=0, concat_axis=0, tiled=True)
    return pl.pallas_call(
        functools.partial(
            output_kernel, query_len=query_len, pairs=pairs, passage_rows=passage_rows
        ),
        out_shape=jax.ShapeDtypeStruct((pairs * (query_len + passage_rows), features), bf16),
        in_specs=[VMEM] * 4,
        out_specs=VMEM,
        compiler_params=pltpu.CompilerParams(vmem_limit_bytes=32 * 1024 * 1024),
        cost_estimate=pl.CostEstimate(
            flops=2 * rows * tensors * 2 * HEAD_DIM * features,
            bytes_accessed=3 * 1024 * 1024,
            transcendentals=0,
        ),
        name="output",
    )(heads, narrow_own, narrow_other, packed)


def solution(mesh):
    fine = Mesh(mesh.devices.reshape([size for _, size in SPLIT]), AXES)
    placed = (
        P(CORPUS, None, TENSOR),
        P(CORPUS, None, TENSOR),
        P(),
        P(CORPUS, None),
        P(CORPUS, None),
        P(TENSOR),
        P(CORPUS, None, TENSOR),
        P(TENSOR, CORPUS),
    )
    return jax.shard_map(
        on_device, mesh=fine, in_specs=placed, out_specs=P(CORPUS, TENSOR), check_vma=False
    )
```

```python
import functools

import jax
import jax.numpy as jnp
from jax import lax
from jax.experimental import pallas as pl
from jax.experimental.pallas import tpu as pltpu
from jax.sharding import Mesh, PartitionSpec as P

HEAD_DIM = 128
ROW_TILE = 16
SPLIT = (("z", 8), ("y", 4), ("c", 2), ("h", 2), ("x", 4))
SIZE = dict(SPLIT)
AXES = tuple(name for name, _ in SPLIT)
CORPUS = ("z", "y", "c")
TENSOR = ("h", "x")
VMEM = pl.BlockSpec(memory_space=pltpu.VMEM)


def attention_kernel(near_ref, far_ref, weight_ref, cos_ref, sin_ref, mask_ref, out_ref, normed_ref, *, gain_row):
    bf16, f32 = jnp.bfloat16, jnp.float32
    spread, highs, groups, rows, part = near_ref.shape
    width = spread * highs * 2 * part
    core = lax.axis_index("c")
    for group in range(groups):
        total = jnp.zeros((rows, HEAD_DIM), f32)
        for ref in (near_ref, far_ref):
            for x in range(spread):
                for h in range(highs):
                    chunk = ref[x, h, group].astype(f32)
                    square = chunk * chunk
                    for lane in range(0, part, HEAD_DIM):
                        total = total + square[:, lane : lane + HEAD_DIM]
        inverse = lax.rsqrt(jnp.sum(total, axis=1, keepdims=True) / width + 1e-05)
        for ref, half in ((near_ref, core), (far_ref, 1 - core)):
            for x in range(spread):
                for h in range(highs):
                    chunk = ref[x, h, group].astype(f32)
                    gain = chunk[gain_row : gain_row + 1, :]
                    begin = pl.multiple_of(((h * spread + x) * 2 + half) * part, part)
                    normed_ref[group * rows : (group + 1) * rows, pl.ds(begin, part)] = (
                        chunk * inverse * gain
                    ).astype(bf16)
    projected = jnp.dot(
        normed_ref[...], weight_ref[:, : 3 * HEAD_DIM], preferred_element_type=f32
    )

    def rotate(inputs):
        return (
            inputs * cos_ref[...] + pltpu.roll(inputs, HEAD_DIM // 2, 1) * sin_ref[...]
        ).astype(bf16)

    for group in range(groups):
        mine = projected[group * rows : (group + 1) * rows]
        queries = rotate(mine[:, :HEAD_DIM])
        keys = rotate(mine[:, HEAD_DIM : 2 * HEAD_DIM])
        values = mine[:, 2 * HEAD_DIM :].astype(bf16)
        scores = lax.dot_general(
            queries, keys, (((1,), (1,)), ((), ())), preferred_element_type=f32
        ) * (1.0 / float(HEAD_DIM) ** 0.5)
        scores = jnp.where(mask_ref[group] > 0, scores, -1e30)
        exponent = jnp.exp(scores - jnp.max(scores, axis=-1, keepdims=True))
        weights = (exponent / jnp.sum(exponent, axis=-1, keepdims=True)).astype(bf16)
        out_ref[group] = jnp.dot(weights, values, preferred_element_type=f32).astype(bf16)


def output_kernel(heads_ref, own_ref, other_ref, near_ref, far_ref, out_ref, *, query_len, pairs, passage_rows):
    bf16, f32 = jnp.bfloat16, jnp.float32
    core = lax.axis_index("c")
    numbers = (((1,), (1,)), ((), ()))
    tensors = heads_ref.shape[0] // 2
    columns = own_ref.shape[0] // tensors
    near, far = near_ref[...], far_ref[...]
    first = core == 0
    final = jnp.concatenate(
        [jnp.where(first, near, far), jnp.where(first, far, near)], axis=1
    ).astype(f32)
    summed = jnp.zeros(final.shape, f32)
    for t in range(tensors):
        block = slice(t * columns, (t + 1) * columns)
        partial_value = lax.dot_general(
            heads_ref[core * tensors + t], own_ref[block], numbers, preferred_element_type=f32
        ) + lax.dot_general(
            heads_ref[(1 - core) * tensors + t], other_ref[block], numbers, preferred_element_type=f32
        )
        summed = summed + partial_value.astype(bf16).astype(f32)
    final = final + summed
    blocks = []
    for pair in range(pairs):
        begin = query_len + pair * passage_rows
        blocks += [final[:query_len], final[begin : begin + passage_rows]]
    out_ref[...] = jnp.concatenate(blocks, axis=0).astype(bf16)


def partner(value, axis, bit):
    return lax.ppermute(value, axis, [(i, i ^ bit) for i in range(SIZE[axis])])


def by_core(mine, got):
    first = lax.axis_index("c") == 0
    return jnp.stack([jnp.where(first, mine, got), jnp.where(first, got, mine)])


def halves(value, part):
    first = lax.axis_index("c") == 0
    low, high = value[..., :part], value[..., part:]
    return jnp.where(first, low, high), jnp.where(first, high, low)


def gather_plane(blocks):
    first = lax.axis_index("c") == 0
    keep = jnp.where(first, blocks[0], blocks[1])
    got = partner(jnp.where(first, blocks[1], blocks[0]), "c", 1)
    pair = by_core(keep, got)
    two = jnp.stack([pair, partner(pair, "y", 2)])
    four = jnp.concatenate([two, partner(two, "y", 1)])
    apart = jnp.arange(SIZE["y"], dtype=jnp.int32) ^ lax.axis_index("y")
    where = (apart % 2) * 2 + apart // 2
    return jnp.take(four, where, axis=0, mode="clip").reshape(-1, blocks.shape[2])


def on_device(
    query_rows,
    corpus_rows,
    passage_length,
    candidate_owner,
    candidate_slot,
    norm_gain,
    project_weight,
    output_weight,
):
    bf16, f32, i32 = jnp.bfloat16, jnp.float32, jnp.int32
    plane = SIZE["y"] * SIZE["c"]
    tensors = SIZE["h"] * SIZE["x"]
    stored, passage_rows, features = corpus_rows.shape
    part = features // 2
    query_len = query_rows.shape[1]
    pairs = candidate_owner.shape[1]
    live = query_len + pairs * passage_rows
    rows = (live // ROW_TILE + 1) * ROW_TILE
    depth = project_weight.shape[0]

    raw = jnp.concatenate([corpus_rows.reshape(-1, features), query_rows[0]], axis=0)
    keep, give = halves(raw, part)
    shared = by_core(keep, partner(give, "c", 1))
    held = shared[:, : stored * passage_rows].reshape(2 * stored, passage_rows, part)
    queries = shared[:, stored * passage_rows :]
    library = lax.all_gather(held, "z", axis=0, tiled=True)

    cells = [(z, q, t) for z in range(SIZE["z"]) for q in range(plane) for t in range(tensors)]
    number = {cell: i for i, cell in enumerate(cells)}
    turn = [(number[(z, q, t)], number[(t, q, z)]) for z, q, t in cells]
    narrow = lax.ppermute(output_weight.T, AXES, turn)
    narrow = narrow.reshape(depth, 2, HEAD_DIM).transpose(1, 0, 2)
    wide = project_weight.reshape(depth, 3, 2, HEAD_DIM).transpose(2, 0, 1, 3)
    wide = wide.reshape(2, depth, 3 * HEAD_DIM)
    weight = gather_plane(jnp.concatenate([wide, narrow], axis=2))

    asked = jnp.concatenate([candidate_owner, candidate_slot], axis=1)
    asked, weight = lax.optimization_barrier((asked, weight))
    weight = lax.all_gather(weight, "z", axis=0, tiled=True)
    asked = lax.all_gather(asked, ("y", "c"), axis=0, tiled=True)
    owner, place = asked[:, :pairs], asked[:, pairs:]
    owner_z, owner_y, owner_c = owner // plane, owner // SIZE["c"] % SIZE["y"], owner % SIZE["c"]
    wanted = ((owner_z * SIZE["c"] + owner_c) * stored + place).reshape(-1)
    outgoing = jnp.take(library, wanted, axis=0, mode="clip")
    arrived = lax.all_to_all(outgoing, "y", split_axis=0, concat_axis=0, tiled=True)

    begin = lax.axis_index("y") * SIZE["c"]
    source = lax.dynamic_slice_in_dim(owner_y, begin, SIZE["c"], axis=0)
    spots = jnp.arange(SIZE["c"] * pairs, dtype=i32).reshape(SIZE["c"], pairs)
    passages = jnp.take(
        arrived, (source * SIZE["c"] * pairs + spots).reshape(-1), axis=0, mode="clip"
    ).reshape(SIZE["c"], pairs, passage_rows, part)
    counts = jnp.take(
        passage_length,
        lax.dynamic_slice_in_dim(owner * stored + place, begin, SIZE["c"], axis=0),
        axis=0,
        mode="clip",
    )
    inside = jnp.arange(passage_rows, dtype=i32) < counts[:, :, None]
    passages = jnp.where(inside[..., None], passages, jnp.zeros((), bf16))
    gain, _ = halves(norm_gain, part)
    packed = jnp.concatenate(
        [
            queries,
            passages.reshape(SIZE["c"], -1, part),
            jnp.broadcast_to(gain, (SIZE["c"], 1, part)),
            jnp.zeros((SIZE["c"], rows - live - 1, part), bf16),
        ],
        axis=1,
    )

    far = partner(packed, "h", 1)
    low = lax.axis_index("h") == 0
    both = jnp.stack([jnp.where(low, packed, far), jnp.where(low, far, packed)])
    spread = jnp.broadcast_to(both[None], (SIZE["x"],) + both.shape)
    near_full = lax.all_to_all(spread, "x", split_axis=0, concat_axis=0, tiled=True)
    far_full = partner(near_full, "c", 1)

    row = jnp.arange(rows, dtype=i32)
    is_query = row < query_len
    slot = jnp.where(is_query, row, query_len + (row - query_len) % passage_rows)
    pair = jnp.where(is_query, -1, (row - query_len) // passage_rows)
    count_of = jnp.concatenate(
        [
            jnp.full((SIZE["c"], query_len), passage_rows, i32),
            jnp.repeat(counts, passage_rows, axis=1),
            jnp.zeros((SIZE["c"], rows - live), i32),
        ],
        axis=1,
    )
    allowed = (slot[None, :] <= slot[:, None])[None] & (
        is_query[None, None, :]
        | (
            (pair[None, :] == pair[:, None])[None]
            & (slot[None, :] < query_len + count_of)[:, None, :]
        )
    )
    half = HEAD_DIM // 2
    frequency = jnp.power(10000.0, -2.0 * jnp.arange(half, dtype=f32) / HEAD_DIM)
    angles = slot.astype(f32)[:, None] * frequency[None, :]
    cosine, sine = jnp.cos(angles), jnp.sin(angles)

    attended = pl.pallas_call(
        functools.partial(attention_kernel, gain_row=live),
        out_shape=jax.ShapeDtypeStruct((SIZE["c"], rows, HEAD_DIM), bf16),
        in_specs=[VMEM] * 6,
        out_specs=VMEM,
        scratch_shapes=[pltpu.VMEM((SIZE["c"] * rows, tensors * features), bf16)],
        compiler_params=pltpu.CompilerParams(vmem_limit_bytes=32 * 1024 * 1024),
        cost_estimate=pl.CostEstimate(
            flops=2 * rows * tensors * features * 6 * HEAD_DIM,
            bytes_accessed=8 * 1024 * 1024,
            transcendentals=2 * rows * rows,
        ),
        name="attention",
    )(
        near_full,
        far_full,
        weight,
        jnp.concatenate([cosine, cosine], axis=1),
        jnp.concatenate([-sine, sine], axis=1),
        allowed.astype(f32),
    )

    spread = jnp.broadcast_to(attended[:, None], (SIZE["c"], tensors, rows, HEAD_DIM))
    heads = lax.all_to_all(
        spread.reshape(-1, rows, HEAD_DIM),
        ("c",) + TENSOR,
        split_axis=0,
        concat_axis=0,
        tiled=True,
    )
    own_out = weight[:, 3 * HEAD_DIM :]
    own_out, _ = lax.optimization_barrier((own_out, attended))
    other_out = partner(own_out, "c", 1)
    core = lax.axis_index("c")
    near_rows = lax.dynamic_index_in_dim(packed, core, axis=0, keepdims=False)
    far_rows = lax.dynamic_slice(
        far_full,
        (lax.axis_index("x"), lax.axis_index("h"), core, 0, 0),
        (1, 1, 1, rows, part),
    ).reshape(rows, part)
    return pl.pallas_call(
        functools.partial(
            output_kernel, query_len=query_len, pairs=pairs, passage_rows=passage_rows
        ),
        out_shape=jax.ShapeDtypeStruct((pairs * (query_len + passage_rows), features), bf16),
        in_specs=[VMEM] * 5,
        out_specs=VMEM,
        compiler_params=pltpu.CompilerParams(vmem_limit_bytes=32 * 1024 * 1024),
        cost_estimate=pl.CostEstimate(
            flops=2 * rows * tensors * 2 * HEAD_DIM * features,
            bytes_accessed=3 * 1024 * 1024,
            transcendentals=0,
        ),
        name="output",
    )(heads, own_out, other_out, near_rows, far_rows)


def solution(mesh):
    fine = Mesh(mesh.devices.reshape([size for _, size in SPLIT]), AXES)
    placed = (
        P(CORPUS, None, TENSOR),
        P(CORPUS, None, TENSOR),
        P(),
        P(CORPUS, None),
        P(CORPUS, None),
        P(TENSOR),
        P(CORPUS, None, TENSOR),
        P(TENSOR, CORPUS),
    )
    return jax.shard_map(
        on_device, mesh=fine, in_specs=placed, out_specs=P(CORPUS, TENSOR), check_vma=False
    )
```

```python
import functools

import jax
import jax.numpy as jnp
import numpy as np
from jax import lax
from jax.experimental import pallas as pl
from jax.experimental.pallas import tpu as pltpu
from jax.sharding import Mesh, PartitionSpec as P

HEAD_DIM = 128
ROW_TILE = 16
SPLIT = (("z", 8), ("y", 4), ("c", 2), ("h", 2), ("x", 4))
SIZE = dict(SPLIT)
AXES = tuple(name for name, _ in SPLIT)
CORPUS = ("z", "y", "c")
TENSOR = ("h", "x")
VMEM = pl.BlockSpec(memory_space=pltpu.VMEM)
SMEM = pl.BlockSpec(memory_space=pltpu.SMEM)
ANY = pl.BlockSpec(memory_space=pl.ANY)
LIMIT = 32 * 1024 * 1024
WEIGHT_PARTS = 4


def pick_kernel(index_ref, library_ref, *out_refs):
    count = out_refs[0].shape[0]
    for block, out_ref in enumerate(out_refs):
        for i in range(count):
            out_ref[i] = library_ref[index_ref[block * count + i]]


def pack_kernel(source_ref, count_ref, *refs):
    f32 = jnp.float32
    part_refs, (query_ref, gain_ref, packed_ref, spread_ref) = refs[:-4], refs[-4:]
    groups, rows, part = packed_ref.shape
    passage_rows = part_refs[0].shape[1]
    pairs = part_refs[0].shape[0] // groups
    place = lax.broadcasted_iota(jnp.int32, (passage_rows, part), 0)
    for group in range(groups):
        blocks = [query_ref[group].astype(f32)]
        for pair in range(pairs):
            spot = group * pairs + pair
            source = source_ref[spot]
            passage = part_refs[0][spot].astype(f32)
            for k in range(1, len(part_refs)):
                passage = jnp.where(source == k, part_refs[k][spot].astype(f32), passage)
            blocks.append(jnp.where(place < count_ref[spot], passage, 0.0))
        filled = blocks[0].shape[0] + pairs * passage_rows
        blocks.append(jnp.broadcast_to(gain_ref[...].astype(f32), (rows - filled, part)))
        value = jnp.concatenate(blocks, axis=0).astype(packed_ref.dtype)
        packed_ref[group] = value
        for x in range(spread_ref.shape[0]):
            spread_ref[x, group] = value


def attention_kernel(
    count_ref, own_ref, far_ref, own_swap_ref, far_swap_ref, weight_ref, cos_ref, sin_ref,
    out_ref, normed_ref, held_ref, semaphores, *, query_len, passage_rows,
):
    bf16, f32, i32 = jnp.bfloat16, jnp.float32, jnp.int32
    spread, groups, rows, part = own_ref.shape
    width = 4 * spread * part
    pairs = count_ref.shape[0] // groups
    gain_row = query_len + pairs * passage_rows
    depth = held_ref.shape[0] // WEIGHT_PARTS
    copies = []
    for i in range(WEIGHT_PARTS):
        block = pl.ds(i * depth, depth)
        copies.append(
            pltpu.make_async_copy(
                weight_ref.at[block, pl.ds(0, held_ref.shape[1])],
                held_ref.at[block],
                semaphores.at[i],
            )
        )
        copies[-1].start()
    core, high = lax.axis_index("c"), lax.axis_index("h")
    quarters = (
        (own_ref, high, core),
        (far_ref, 1 - high, core),
        (own_swap_ref, high, 1 - core),
        (far_swap_ref, 1 - high, 1 - core),
    )
    for group in range(groups):
        total = jnp.zeros((rows, HEAD_DIM), f32)
        for ref, _, _ in quarters:
            for x in range(spread):
                chunk = ref[x, group].astype(f32)
                square = chunk * chunk
                for lane in range(0, part, HEAD_DIM):
                    total = total + square[:, lane : lane + HEAD_DIM]
        inverse = lax.rsqrt(jnp.sum(total, axis=1, keepdims=True) / width + 1e-05)
        for ref, upper, half in quarters:
            for x in range(spread):
                chunk = ref[x, group].astype(f32)
                gain = chunk[gain_row : gain_row + 1, :]
                begin = pl.multiple_of(((upper * spread + x) * 2 + half) * part, part)
                normed_ref[group * rows : (group + 1) * rows, pl.ds(begin, part)] = (
                    chunk * inverse * gain
                ).astype(bf16)
    projected = None
    for i in range(WEIGHT_PARTS):
        copies[i].wait()
        block = slice(i * depth, (i + 1) * depth)
        product = jnp.dot(normed_ref[:, block], held_ref[block], preferred_element_type=f32)
        projected = product if projected is None else projected + product

    def rotate(inputs):
        return (
            inputs * cos_ref[...] + pltpu.roll(inputs, HEAD_DIM // 2, 1) * sin_ref[...]
        ).astype(bf16)

    def pair_of(row):
        pair = jnp.full(row.shape, -1, i32)
        for k in range(pairs + 1):
            pair = jnp.where(row >= query_len + k * passage_rows, k, pair)
        return pair

    query_row = lax.broadcasted_iota(i32, (rows, 1), 0)
    key_row = lax.broadcasted_iota(i32, (1, rows), 1)
    query_pair, key_pair = pair_of(query_row), pair_of(key_row)
    for group in range(groups):
        end = jnp.full((1, rows), query_len, i32)
        for k in range(pairs):
            last = query_len + k * passage_rows + count_ref[group * pairs + k]
            end = jnp.where(key_pair == k, last, end)
        key_live = jnp.where(key_row < end, key_pair, -2)
        allowed = (key_row <= query_row) & ((key_live == -1) | (key_live == query_pair))
        mine = projected[group * rows : (group + 1) * rows]
        queries = rotate(mine[:, :HEAD_DIM])
        keys = rotate(mine[:, HEAD_DIM : 2 * HEAD_DIM])
        values = mine[:, 2 * HEAD_DIM :].astype(bf16)
        scores = lax.dot_general(
            queries, keys, (((1,), (1,)), ((), ())), preferred_element_type=f32
        ) * (1.0 / float(HEAD_DIM) ** 0.5)
        scores = jnp.where(allowed, scores, -1e30)
        exponent = jnp.exp(scores - jnp.max(scores, axis=-1, keepdims=True))
        weights = (exponent / jnp.sum(exponent, axis=-1, keepdims=True)).astype(bf16)
        attended = jnp.dot(weights, values, preferred_element_type=f32).astype(bf16)
        for t in range(out_ref.shape[1]):
            out_ref[group, t] = attended


def output_kernel(heads_ref, own_ref, other_ref, near_ref, far_ref, out_ref, *, query_len, pairs, passage_rows):
    bf16, f32 = jnp.bfloat16, jnp.float32
    core = lax.axis_index("c")
    numbers = (((1,), (1,)), ((), ()))
    tensors = heads_ref.shape[0] // 2
    columns = own_ref.shape[0] // tensors
    near, far = near_ref[...], far_ref[...]
    first = core == 0
    final = jnp.concatenate(
        [jnp.where(first, near, far), jnp.where(first, far, near)], axis=1
    ).astype(f32)
    summed = jnp.zeros(final.shape, f32)
    for t in range(tensors):
        block = slice(t * columns, (t + 1) * columns)
        partial_value = lax.dot_general(
            heads_ref[core * tensors + t], own_ref[block], numbers, preferred_element_type=f32
        ) + lax.dot_general(
            heads_ref[(1 - core) * tensors + t], other_ref[block], numbers, preferred_element_type=f32
        )
        summed = summed + partial_value.astype(bf16).astype(f32)
    final = final + summed
    blocks = []
    for pair in range(pairs):
        begin = query_len + pair * passage_rows
        blocks += [final[:query_len], final[begin : begin + passage_rows]]
    out_ref[...] = jnp.concatenate(blocks, axis=0).astype(bf16)


def partner(value, axis, bit):
    return lax.ppermute(value, axis, [(i, i ^ bit) for i in range(SIZE[axis])])


def by_core(mine, got):
    first = lax.axis_index("c") == 0
    return jnp.stack([jnp.where(first, mine, got), jnp.where(first, got, mine)])


def halves(value, part):
    first = lax.axis_index("c") == 0
    low, high = value[..., :part], value[..., part:]
    return jnp.where(first, low, high), jnp.where(first, high, low)


def gather_plane(blocks):
    first = lax.axis_index("c") == 0
    keep = jnp.where(first, blocks[0], blocks[1])
    got = partner(jnp.where(first, blocks[1], blocks[0]), "c", 1)
    pair = by_core(keep, got)
    four = jnp.stack([pair] + [partner(pair, "y", k) for k in range(1, SIZE["y"])])
    return jnp.take(four, other_y(), axis=0, mode="clip")


def other_y():
    return jnp.arange(SIZE["y"], dtype=jnp.int32) ^ lax.axis_index("y")


def on_every(value, axis):
    spread = jnp.broadcast_to(value[None], (SIZE[axis],) + value.shape)
    return lax.all_to_all(spread, axis, split_axis=0, concat_axis=0, tiled=True)


def on_device(
    query_rows,
    corpus_rows,
    passage_length,
    candidate_owner,
    candidate_slot,
    norm_gain,
    project_weight,
    output_weight,
):
    bf16, f32, i32 = jnp.bfloat16, jnp.float32, jnp.int32
    cores, lines = SIZE["c"], SIZE["y"]
    plane = lines * cores
    tensors = SIZE["h"] * SIZE["x"]
    stored, passage_rows, features = corpus_rows.shape
    part = features // 2
    query_len = query_rows.shape[1]
    pairs = candidate_owner.shape[1]
    live = query_len + pairs * passage_rows
    rows = (live // ROW_TILE + 1) * ROW_TILE
    depth = project_weight.shape[0]
    options = pltpu.CompilerParams(vmem_limit_bytes=LIMIT)

    raw = jnp.concatenate([corpus_rows.reshape(-1, features), query_rows[0]], axis=0)
    keep, give = halves(raw, part)
    shared = by_core(keep, partner(give, "c", 1))
    held = shared[:, : stored * passage_rows].reshape(2 * stored, passage_rows, part)
    queries = shared[:, stored * passage_rows :]
    library = on_every(held, "z").reshape(-1, passage_rows, part)

    cells = [(z, q, t) for z in range(SIZE["z"]) for q in range(plane) for t in range(tensors)]
    number = {cell: i for i, cell in enumerate(cells)}
    turn = [(number[(z, q, t)], number[(t, q, z)]) for z, q, t in cells]
    narrow = lax.ppermute(output_weight.T, AXES, turn)
    narrow = narrow.reshape(depth, 2, HEAD_DIM).transpose(1, 0, 2)
    wide = project_weight.reshape(depth, 3, 2, HEAD_DIM).transpose(2, 0, 1, 3)
    wide = wide.reshape(2, depth, 3 * HEAD_DIM)
    asked = jnp.concatenate([candidate_owner, candidate_slot], axis=1).astype(bf16)
    asked = jnp.pad(asked, ((0, 7), (0, 4 * HEAD_DIM - 2 * pairs)))
    weight = jnp.concatenate([wide, narrow], axis=2)
    weight = jnp.concatenate([weight, jnp.broadcast_to(asked, (2,) + asked.shape)], axis=1)
    weight = gather_plane(weight)
    asked = weight[:, :, depth, : 2 * pairs].astype(i32)
    weight = weight[:, :, :depth].reshape(plane * depth, 4 * HEAD_DIM)
    weight = lax.all_gather(weight, "z", axis=0, tiled=True)

    owner, place = asked[:, :, :pairs], asked[:, :, pairs:]
    owner_z, owner_y, owner_c = owner // plane, owner // cores % lines, owner % cores
    wanted = (owner_z * cores + owner_c) * stored + place
    wanted = jnp.take(wanted, other_y(), axis=0, mode="clip").reshape(-1)
    block = jax.ShapeDtypeStruct((cores * pairs, passage_rows, part), bf16)
    outgoing = pl.pallas_call(
        pick_kernel,
        out_shape=[block] * lines,
        in_specs=[SMEM, VMEM],
        out_specs=[VMEM] * lines,
        compiler_params=options,
        name="pick",
    )(wanted, library)
    arrived = [outgoing[0]] + [partner(outgoing[k], "y", k) for k in range(1, lines)]

    here = lax.axis_index("y")
    source = lax.dynamic_index_in_dim(owner_y, here, axis=0, keepdims=False) ^ here
    stored_at = lax.dynamic_index_in_dim(owner * stored + place, here, axis=0, keepdims=False)
    counts = jnp.take(passage_length, stored_at.reshape(-1), axis=0, mode="clip")
    gain, _ = halves(norm_gain[None], part)
    packed, spread = pl.pallas_call(
        pack_kernel,
        out_shape=[
            jax.ShapeDtypeStruct((cores, rows, part), bf16),
            jax.ShapeDtypeStruct((SIZE["x"], cores, rows, part), bf16),
        ],
        in_specs=[SMEM] * 2 + [VMEM] * (lines + 2),
        out_specs=[VMEM] * 2,
        compiler_params=options,
        name="pack",
    )(source.reshape(-1), counts, *arrived, queries, gain)

    own_full = lax.all_to_all(spread, "x", split_axis=0, concat_axis=0, tiled=True)
    far_full = on_every(partner(packed, "h", 1), "x")
    own_swap = partner(own_full, "c", 1)
    far_swap = partner(far_full, "c", 1)

    row = np.arange(rows)
    slot = np.where(row < query_len, row, query_len + (row - query_len) % passage_rows)
    half = HEAD_DIM // 2
    frequency = np.power(10000.0, -2.0 * np.arange(half) / HEAD_DIM).astype(np.float32)
    angles = slot.astype(np.float32)[:, None] * frequency[None, :]
    cosine, sine = np.cos(angles), np.sin(angles)
    attended = pl.pallas_call(
        functools.partial(attention_kernel, query_len=query_len, passage_rows=passage_rows),
        out_shape=jax.ShapeDtypeStruct((cores, tensors, rows, HEAD_DIM), bf16),
        in_specs=[SMEM] + [VMEM] * 4 + [ANY] + [VMEM] * 2,
        out_specs=VMEM,
        scratch_shapes=[
            pltpu.VMEM((cores * rows, tensors * features), bf16),
            pltpu.VMEM((weight.shape[0], 3 * HEAD_DIM), bf16),
            pltpu.SemaphoreType.DMA((WEIGHT_PARTS,)),
        ],
        compiler_params=options,
        cost_estimate=pl.CostEstimate(
            flops=2 * rows * tensors * features * 6 * HEAD_DIM,
            bytes_accessed=8 * 1024 * 1024,
            transcendentals=2 * rows * rows,
        ),
        name="attention",
    )(
        counts,
        own_full,
        far_full,
        own_swap,
        far_swap,
        weight,
        jnp.asarray(np.concatenate([cosine, cosine], axis=1), f32),
        jnp.asarray(np.concatenate([-sine, sine], axis=1), f32),
    )

    heads = lax.all_to_all(
        attended.reshape(-1, rows, HEAD_DIM),
        ("c",) + TENSOR,
        split_axis=0,
        concat_axis=0,
        tiled=True,
    )
    own_out = weight[:, 3 * HEAD_DIM :]
    own_out, _ = lax.optimization_barrier((own_out, attended))
    other_out = partner(own_out, "c", 1)
    core = lax.axis_index("c")
    near_rows = lax.dynamic_index_in_dim(packed, core, axis=0, keepdims=False)
    far_rows = lax.dynamic_slice(
        own_swap, (lax.axis_index("x"), core, 0, 0), (1, 1, rows, part)
    ).reshape(rows, part)
    return pl.pallas_call(
        functools.partial(
            output_kernel, query_len=query_len, pairs=pairs, passage_rows=passage_rows
        ),
        out_shape=jax.ShapeDtypeStruct((pairs * (query_len + passage_rows), features), bf16),
        in_specs=[VMEM] * 5,
        out_specs=VMEM,
        compiler_params=options,
        cost_estimate=pl.CostEstimate(
            flops=2 * rows * tensors * 2 * HEAD_DIM * features,
            bytes_accessed=3 * 1024 * 1024,
            transcendentals=0,
        ),
        name="output",
    )(heads, own_out, other_out, near_rows, far_rows)


def solution(mesh):
    fine = Mesh(mesh.devices.reshape([size for _, size in SPLIT]), AXES)
    placed = (
        P(CORPUS, None, TENSOR),
        P(CORPUS, None, TENSOR),
        P(),
        P(CORPUS, None),
        P(CORPUS, None),
        P(TENSOR),
        P(CORPUS, None, TENSOR),
        P(TENSOR, CORPUS),
    )
    return jax.shard_map(
        on_device, mesh=fine, in_specs=placed, out_specs=P(CORPUS, TENSOR), check_vma=False
    )
```

```python
import functools

import jax
import jax.numpy as jnp
import numpy as np
from jax import lax
from jax.experimental import pallas as pl
from jax.experimental.pallas import tpu as pltpu
from jax.sharding import Mesh, PartitionSpec as P

HEAD_DIM = 128
ROW_TILE = 16
SPLIT = (("z", 8), ("y", 4), ("c", 2), ("h", 2), ("x", 4))
SIZE = dict(SPLIT)
AXES = tuple(name for name, _ in SPLIT)
CORPUS = ("z", "y", "c")
TENSOR = ("h", "x")
VMEM = pl.BlockSpec(memory_space=pltpu.VMEM)
SMEM = pl.BlockSpec(memory_space=pltpu.SMEM)
MIB = 1024 * 1024


def pick_kernel(index_ref, library_ref, *out_refs):
    count = out_refs[0].shape[0]
    for block, out_ref in enumerate(out_refs):
        for i in range(count):
            out_ref[i] = library_ref[index_ref[block * count + i]]


def pack_kernel(source_ref, count_ref, *refs):
    f32 = jnp.float32
    part_refs, (query_ref, gain_ref, packed_ref, spread_ref) = refs[:-4], refs[-4:]
    groups, rows, part = packed_ref.shape
    passage_rows = part_refs[0].shape[1]
    pairs = part_refs[0].shape[0] // groups
    place = lax.broadcasted_iota(jnp.int32, (passage_rows, part), 0)
    for group in range(groups):
        blocks = [query_ref[group].astype(f32)]
        for pair in range(pairs):
            spot = group * pairs + pair
            source = source_ref[spot]
            passage = part_refs[0][spot].astype(f32)
            for k in range(1, len(part_refs)):
                passage = jnp.where(source == k, part_refs[k][spot].astype(f32), passage)
            blocks.append(jnp.where(place < count_ref[spot], passage, 0.0))
        filled = blocks[0].shape[0] + pairs * passage_rows
        blocks.append(jnp.broadcast_to(gain_ref[...].astype(f32), (rows - filled, part)))
        value = jnp.concatenate(blocks, axis=0).astype(packed_ref.dtype)
        packed_ref[group] = value
        for x in range(spread_ref.shape[0]):
            spread_ref[x, group] = value


def attention_kernel(
    count_ref, own_ref, far_ref, own_swap_ref, far_swap_ref, weight_ref, cos_ref, sin_ref,
    out_ref, normed_ref, *, query_len, passage_rows,
):
    bf16, f32, i32 = jnp.bfloat16, jnp.float32, jnp.int32
    spread, groups, rows, part = own_ref.shape
    width = 4 * spread * part
    pairs = count_ref.shape[0] // groups
    gain_row = query_len + pairs * passage_rows
    core, high = lax.axis_index("c"), lax.axis_index("h")
    quarters = (
        (own_ref, high, core),
        (far_ref, 1 - high, core),
        (own_swap_ref, high, 1 - core),
        (far_swap_ref, 1 - high, 1 - core),
    )
    for group in range(groups):
        total = jnp.zeros((rows, HEAD_DIM), f32)
        for ref, _, _ in quarters:
            for x in range(spread):
                chunk = ref[x, group].astype(f32)
                square = chunk * chunk
                for lane in range(0, part, HEAD_DIM):
                    total = total + square[:, lane : lane + HEAD_DIM]
        inverse = lax.rsqrt(jnp.sum(total, axis=1, keepdims=True) / width + 1e-05)
        for ref, upper, half in quarters:
            for x in range(spread):
                chunk = ref[x, group].astype(f32)
                gain = chunk[gain_row : gain_row + 1, :]
                begin = pl.multiple_of(((upper * spread + x) * 2 + half) * part, part)
                normed_ref[group * rows : (group + 1) * rows, pl.ds(begin, part)] = (
                    chunk * inverse * gain
                ).astype(bf16)
    projected = jnp.dot(
        normed_ref[...], weight_ref[:, : 3 * HEAD_DIM], preferred_element_type=f32
    )

    def rotate(inputs):
        return (
            inputs * cos_ref[...] + pltpu.roll(inputs, HEAD_DIM // 2, 1) * sin_ref[...]
        ).astype(bf16)

    def pair_of(row):
        pair = jnp.full(row.shape, -1, i32)
        for k in range(pairs + 1):
            pair = jnp.where(row >= query_len + k * passage_rows, k, pair)
        return pair

    query_row = lax.broadcasted_iota(i32, (rows, 1), 0)
    key_row = lax.broadcasted_iota(i32, (1, rows), 1)
    query_pair, key_pair = pair_of(query_row), pair_of(key_row)
    for group in range(groups):
        end = jnp.full((1, rows), query_len, i32)
        for k in range(pairs):
            last = query_len + k * passage_rows + count_ref[group * pairs + k]
            end = jnp.where(key_pair == k, last, end)
        key_live = jnp.where(key_row < end, key_pair, -2)
        allowed = (key_row <= query_row) & ((key_live == -1) | (key_live == query_pair))
        mine = projected[group * rows : (group + 1) * rows]
        queries = rotate(mine[:, :HEAD_DIM])
        keys = rotate(mine[:, HEAD_DIM : 2 * HEAD_DIM])
        values = mine[:, 2 * HEAD_DIM :].astype(bf16)
        scores = lax.dot_general(
            queries, keys, (((1,), (1,)), ((), ())), preferred_element_type=f32
        ) * (1.0 / float(HEAD_DIM) ** 0.5)
        scores = jnp.where(allowed, scores, -1e30)
        exponent = jnp.exp(scores - jnp.max(scores, axis=-1, keepdims=True))
        weights = (exponent / jnp.sum(exponent, axis=-1, keepdims=True)).astype(bf16)
        attended = jnp.dot(weights, values, preferred_element_type=f32).astype(bf16)
        for t in range(out_ref.shape[1]):
            out_ref[group, t] = attended


def output_kernel(heads_ref, own_ref, other_ref, near_ref, far_ref, out_ref, *, query_len, pairs, passage_rows):
    bf16, f32 = jnp.bfloat16, jnp.float32
    core = lax.axis_index("c")
    numbers = (((1,), (1,)), ((), ()))
    tensors = heads_ref.shape[0] // 2
    columns = own_ref.shape[0] // tensors
    near, far = near_ref[...], far_ref[...]
    first = core == 0
    final = jnp.concatenate(
        [jnp.where(first, near, far), jnp.where(first, far, near)], axis=1
    ).astype(f32)
    summed = jnp.zeros(final.shape, f32)
    for t in range(tensors):
        block = slice(t * columns, (t + 1) * columns)
        partial_value = lax.dot_general(
            heads_ref[core * tensors + t], own_ref[block], numbers, preferred_element_type=f32
        ) + lax.dot_general(
            heads_ref[(1 - core) * tensors + t], other_ref[block], numbers, preferred_element_type=f32
        )
        summed = summed + partial_value.astype(bf16).astype(f32)
    final = final + summed
    blocks = []
    for pair in range(pairs):
        begin = query_len + pair * passage_rows
        blocks += [final[:query_len], final[begin : begin + passage_rows]]
    out_ref[...] = jnp.concatenate(blocks, axis=0).astype(bf16)


def partner(value, axis, bit):
    return lax.ppermute(value, axis, [(i, i ^ bit) for i in range(SIZE[axis])])


def by_core(mine, got):
    first = lax.axis_index("c") == 0
    return jnp.stack([jnp.where(first, mine, got), jnp.where(first, got, mine)])


def halves(value, part):
    first = lax.axis_index("c") == 0
    low, high = value[..., :part], value[..., part:]
    return jnp.where(first, low, high), jnp.where(first, high, low)


def gather_plane(blocks):
    first = lax.axis_index("c") == 0
    keep = jnp.where(first, blocks[0], blocks[1])
    got = partner(jnp.where(first, blocks[1], blocks[0]), "c", 1)
    pair = by_core(keep, got)
    four = jnp.stack([pair] + [partner(pair, "y", k) for k in range(1, SIZE["y"])])
    return jnp.take(four, other_y(), axis=0, mode="clip")


def other_y():
    return jnp.arange(SIZE["y"], dtype=jnp.int32) ^ lax.axis_index("y")


def on_every(value, axis):
    spread = jnp.broadcast_to(value[None], (SIZE[axis],) + value.shape)
    return lax.all_to_all(spread, axis, split_axis=0, concat_axis=0, tiled=True)


def on_device(
    query_rows,
    corpus_rows,
    passage_length,
    candidate_owner,
    candidate_slot,
    norm_gain,
    project_weight,
    output_weight,
):
    bf16, f32, i32 = jnp.bfloat16, jnp.float32, jnp.int32
    cores, lines = SIZE["c"], SIZE["y"]
    plane = lines * cores
    tensors = SIZE["h"] * SIZE["x"]
    stored, passage_rows, features = corpus_rows.shape
    part = features // 2
    query_len = query_rows.shape[1]
    pairs = candidate_owner.shape[1]
    live = query_len + pairs * passage_rows
    rows = (live // ROW_TILE + 1) * ROW_TILE
    depth = project_weight.shape[0]
    options = pltpu.CompilerParams(vmem_limit_bytes=8 * MIB)

    raw = jnp.concatenate([corpus_rows.reshape(-1, features), query_rows[0]], axis=0)
    keep, give = halves(raw, part)
    shared = by_core(keep, partner(give, "c", 1))
    held = shared[:, : stored * passage_rows].reshape(2 * stored, passage_rows, part)
    queries = shared[:, stored * passage_rows :]
    output_weight, project_weight, held = lax.optimization_barrier(
        (output_weight, project_weight, held)
    )
    library = lax.all_gather(held, "z", axis=0, tiled=True)

    cells = [(z, q, t) for z in range(SIZE["z"]) for q in range(plane) for t in range(tensors)]
    number = {cell: i for i, cell in enumerate(cells)}
    turn = [(number[(z, q, t)], number[(t, q, z)]) for z, q, t in cells]
    narrow = lax.ppermute(output_weight.T, AXES, turn)
    narrow = narrow.reshape(depth, 2, HEAD_DIM).transpose(1, 0, 2)
    wide = project_weight.reshape(depth, 3, 2, HEAD_DIM).transpose(2, 0, 1, 3)
    wide = wide.reshape(2, depth, 3 * HEAD_DIM)
    asked = jnp.concatenate([candidate_owner, candidate_slot], axis=1).astype(bf16)
    asked = jnp.pad(asked, ((0, 7), (0, 4 * HEAD_DIM - 2 * pairs)))
    weight = jnp.concatenate([wide, narrow], axis=2)
    weight = jnp.concatenate([weight, jnp.broadcast_to(asked, (2,) + asked.shape)], axis=1)
    weight = gather_plane(weight)
    asked = weight[:, :, depth, : 2 * pairs].astype(i32)
    weight = weight[:, :, :depth].reshape(plane * depth, 4 * HEAD_DIM)
    weight = lax.all_gather(weight, "z", axis=0, tiled=True)

    owner, place = asked[:, :, :pairs], asked[:, :, pairs:]
    owner_z, owner_y, owner_c = owner // plane, owner // cores % lines, owner % cores
    wanted = (owner_z * cores + owner_c) * stored + place
    wanted = jnp.take(wanted, other_y(), axis=0, mode="clip").reshape(-1)
    block = jax.ShapeDtypeStruct((cores * pairs, passage_rows, part), bf16)
    outgoing = pl.pallas_call(
        pick_kernel,
        out_shape=[block] * lines,
        in_specs=[SMEM, VMEM],
        out_specs=[VMEM] * lines,
        compiler_params=options,
        name="pick",
    )(wanted, library)
    arrived = [outgoing[0]] + [partner(outgoing[k], "y", k) for k in range(1, lines)]

    here = lax.axis_index("y")
    source = lax.dynamic_index_in_dim(owner_y, here, axis=0, keepdims=False) ^ here
    stored_at = lax.dynamic_index_in_dim(owner * stored + place, here, axis=0, keepdims=False)
    counts = jnp.take(passage_length, stored_at.reshape(-1), axis=0, mode="clip")
    gain, _ = halves(norm_gain[None], part)
    packed, spread = pl.pallas_call(
        pack_kernel,
        out_shape=[
            jax.ShapeDtypeStruct((cores, rows, part), bf16),
            jax.ShapeDtypeStruct((SIZE["x"], cores, rows, part), bf16),
        ],
        in_specs=[SMEM] * 2 + [VMEM] * (lines + 2),
        out_specs=[VMEM] * 2,
        compiler_params=options,
        name="pack",
    )(source.reshape(-1), counts, *arrived, queries, gain)

    own_full = lax.all_to_all(spread, "x", split_axis=0, concat_axis=0, tiled=True)
    far_full = on_every(partner(packed, "h", 1), "x")
    own_swap = partner(own_full, "c", 1)
    far_swap = partner(far_full, "c", 1)

    row = np.arange(rows)
    slot = np.where(row < query_len, row, query_len + (row - query_len) % passage_rows)
    half = HEAD_DIM // 2
    frequency = np.power(10000.0, -2.0 * np.arange(half) / HEAD_DIM).astype(np.float32)
    angles = slot.astype(np.float32)[:, None] * frequency[None, :]
    cosine, sine = np.cos(angles), np.sin(angles)
    attended = pl.pallas_call(
        functools.partial(attention_kernel, query_len=query_len, passage_rows=passage_rows),
        out_shape=jax.ShapeDtypeStruct((cores, tensors, rows, HEAD_DIM), bf16),
        in_specs=[SMEM] + [VMEM] * 7,
        out_specs=VMEM,
        scratch_shapes=[pltpu.VMEM((cores * rows, tensors * features), bf16)],
        compiler_params=pltpu.CompilerParams(vmem_limit_bytes=24 * MIB),
        cost_estimate=pl.CostEstimate(
            flops=2 * rows * tensors * features * 6 * HEAD_DIM,
            bytes_accessed=8 * 1024 * 1024,
            transcendentals=2 * rows * rows,
        ),
        name="attention",
    )(
        counts,
        own_full,
        far_full,
        own_swap,
        far_swap,
        weight,
        jnp.asarray(np.concatenate([cosine, cosine], axis=1), f32),
        jnp.asarray(np.concatenate([-sine, sine], axis=1), f32),
    )

    heads = lax.all_to_all(
        attended.reshape(-1, rows, HEAD_DIM),
        ("c",) + TENSOR,
        split_axis=0,
        concat_axis=0,
        tiled=True,
    )
    own_out = weight[:, 3 * HEAD_DIM :]
    own_out, _ = lax.optimization_barrier((own_out, attended))
    other_out = partner(own_out, "c", 1)
    core = lax.axis_index("c")
    near_rows = lax.dynamic_index_in_dim(packed, core, axis=0, keepdims=False)
    far_rows = lax.dynamic_slice(
        own_swap, (lax.axis_index("x"), core, 0, 0), (1, 1, rows, part)
    ).reshape(rows, part)
    return pl.pallas_call(
        functools.partial(
            output_kernel, query_len=query_len, pairs=pairs, passage_rows=passage_rows
        ),
        out_shape=jax.ShapeDtypeStruct((pairs * (query_len + passage_rows), features), bf16),
        in_specs=[VMEM] * 5,
        out_specs=VMEM,
        compiler_params=options,
        cost_estimate=pl.CostEstimate(
            flops=2 * rows * tensors * 2 * HEAD_DIM * features,
            bytes_accessed=3 * 1024 * 1024,
            transcendentals=0,
        ),
        name="output",
    )(heads, own_out, other_out, near_rows, far_rows)


def solution(mesh):
    fine = Mesh(mesh.devices.reshape([size for _, size in SPLIT]), AXES)
    placed = (
        P(CORPUS, None, TENSOR),
        P(CORPUS, None, TENSOR),
        P(),
        P(CORPUS, None),
        P(CORPUS, None),
        P(TENSOR),
        P(CORPUS, None, TENSOR),
        P(TENSOR, CORPUS),
    )
    return jax.shard_map(
        on_device, mesh=fine, in_specs=placed, out_specs=P(CORPUS, TENSOR), check_vma=False
    )
```

```python
import functools

import jax
import jax.numpy as jnp
import numpy as np
from jax import lax
from jax.experimental import pallas as pl
from jax.experimental.pallas import tpu as pltpu
from jax.sharding import Mesh, PartitionSpec as P

HEAD_DIM = 128
ROW_TILE = 16
SPLIT = (("z", 8), ("y", 4), ("c", 2), ("h", 2), ("x", 4))
SIZE = dict(SPLIT)
AXES = tuple(name for name, _ in SPLIT)
CORPUS = ("z", "y", "c")
TENSOR = ("h", "x")
VMEM = pl.BlockSpec(memory_space=pltpu.VMEM)
SMEM = pl.BlockSpec(memory_space=pltpu.SMEM)
MIB = 1024 * 1024


def pick_kernel(index_ref, library_ref, *out_refs):
    count = out_refs[0].shape[0]
    for block, out_ref in enumerate(out_refs):
        for i in range(count):
            out_ref[i] = library_ref[index_ref[block * count + i]]


def pack_kernel(source_ref, count_ref, *refs):
    f32 = jnp.float32
    part_refs, (query_ref, gain_ref, packed_ref) = refs[:-3], refs[-3:]
    groups, rows, part = packed_ref.shape
    passage_rows = part_refs[0].shape[1]
    pairs = part_refs[0].shape[0] // groups
    place = lax.broadcasted_iota(jnp.int32, (passage_rows, part), 0)
    for group in range(groups):
        blocks = [query_ref[group].astype(f32)]
        for pair in range(pairs):
            spot = group * pairs + pair
            source = source_ref[spot]
            passage = part_refs[0][spot].astype(f32)
            for k in range(1, len(part_refs)):
                passage = jnp.where(source == k, part_refs[k][spot].astype(f32), passage)
            blocks.append(jnp.where(place < count_ref[spot], passage, 0.0))
        filled = blocks[0].shape[0] + pairs * passage_rows
        blocks.append(jnp.broadcast_to(gain_ref[...].astype(f32), (rows - filled, part)))
        packed_ref[group] = jnp.concatenate(blocks, axis=0).astype(packed_ref.dtype)


def norm_kernel(own_ref, far_ref, own_swap_ref, far_swap_ref, normed_ref, *, gain_row):
    bf16, f32 = jnp.bfloat16, jnp.float32
    spread, groups, rows, part = own_ref.shape
    width = 4 * spread * part
    core, high = lax.axis_index("c"), lax.axis_index("h")
    quarters = (
        (own_ref, high, core),
        (far_ref, 1 - high, core),
        (own_swap_ref, high, 1 - core),
        (far_swap_ref, 1 - high, 1 - core),
    )
    for group in range(groups):
        total = jnp.zeros((rows, HEAD_DIM), f32)
        for ref, _, _ in quarters:
            for x in range(spread):
                chunk = ref[x, group].astype(f32)
                square = chunk * chunk
                for lane in range(0, part, HEAD_DIM):
                    total = total + square[:, lane : lane + HEAD_DIM]
        inverse = lax.rsqrt(jnp.sum(total, axis=1, keepdims=True) / width + 1e-05)
        for ref, upper, half in quarters:
            for x in range(spread):
                chunk = ref[x, group].astype(f32)
                gain = chunk[gain_row : gain_row + 1, :]
                begin = pl.multiple_of(((upper * spread + x) * 2 + half) * part, part)
                normed_ref[group * rows : (group + 1) * rows, pl.ds(begin, part)] = (
                    chunk * inverse * gain
                ).astype(bf16)


def attention_kernel(
    count_ref, normed_ref, weight_ref, cos_ref, sin_ref, out_ref, spread_ref, *, query_len, passage_rows
):
    bf16, f32, i32 = jnp.bfloat16, jnp.float32, jnp.int32
    groups, rows, _ = out_ref.shape
    pairs = count_ref.shape[0] // groups
    projected = jnp.dot(
        normed_ref[...], weight_ref[:, : 3 * HEAD_DIM], preferred_element_type=f32
    )

    def rotate(inputs):
        return (
            inputs * cos_ref[...] + pltpu.roll(inputs, HEAD_DIM // 2, 1) * sin_ref[...]
        ).astype(bf16)

    def pair_of(row):
        pair = jnp.full(row.shape, -1, i32)
        for k in range(pairs + 1):
            pair = jnp.where(row >= query_len + k * passage_rows, k, pair)
        return pair

    query_row = lax.broadcasted_iota(i32, (rows, 1), 0)
    key_row = lax.broadcasted_iota(i32, (1, rows), 1)
    query_pair, key_pair = pair_of(query_row), pair_of(key_row)
    for group in range(groups):
        end = jnp.full((1, rows), query_len, i32)
        for k in range(pairs):
            last = query_len + k * passage_rows + count_ref[group * pairs + k]
            end = jnp.where(key_pair == k, last, end)
        key_live = jnp.where(key_row < end, key_pair, -2)
        allowed = (key_row <= query_row) & ((key_live == -1) | (key_live == query_pair))
        mine = projected[group * rows : (group + 1) * rows]
        queries = rotate(mine[:, :HEAD_DIM])
        keys = rotate(mine[:, HEAD_DIM : 2 * HEAD_DIM])
        values = mine[:, 2 * HEAD_DIM :].astype(bf16)
        scores = lax.dot_general(
            queries, keys, (((1,), (1,)), ((), ())), preferred_element_type=f32
        ) * (1.0 / float(HEAD_DIM) ** 0.5)
        scores = jnp.where(allowed, scores, -1e30)
        exponent = jnp.exp(scores - jnp.max(scores, axis=-1, keepdims=True))
        weights = (exponent / jnp.sum(exponent, axis=-1, keepdims=True)).astype(bf16)
        attended = jnp.dot(weights, values, preferred_element_type=f32).astype(bf16)
        out_ref[group] = attended
        for x in range(spread_ref.shape[1]):
            spread_ref[group, x] = attended


def output_kernel(own_heads_ref, far_heads_ref, own_ref, other_ref, near_ref, far_ref, out_ref, *, query_len, pairs, passage_rows):
    bf16, f32 = jnp.bfloat16, jnp.float32
    core = lax.axis_index("c")
    numbers = (((1,), (1,)), ((), ()))
    spread = own_heads_ref.shape[0] // 2
    columns = own_ref.shape[0] // (2 * spread)
    near, far = near_ref[...], far_ref[...]
    first = core == 0
    final = jnp.concatenate(
        [jnp.where(first, near, far), jnp.where(first, far, near)], axis=1
    ).astype(f32)
    summed = jnp.zeros(final.shape, f32)
    high = lax.axis_index("h")
    for heads_ref, upper in ((own_heads_ref, high), (far_heads_ref, 1 - high)):
        for x in range(spread):
            block = pl.ds(pl.multiple_of((upper * spread + x) * columns, columns), columns)
            partial_value = lax.dot_general(
                heads_ref[core * spread + x], own_ref[block], numbers, preferred_element_type=f32
            ) + lax.dot_general(
                heads_ref[(1 - core) * spread + x], other_ref[block], numbers, preferred_element_type=f32
            )
            summed = summed + partial_value.astype(bf16).astype(f32)
    final = final + summed
    blocks = []
    for pair in range(pairs):
        begin = query_len + pair * passage_rows
        blocks += [final[:query_len], final[begin : begin + passage_rows]]
    out_ref[...] = jnp.concatenate(blocks, axis=0).astype(bf16)


def partner(value, axis, bit):
    return lax.ppermute(value, axis, [(i, i ^ bit) for i in range(SIZE[axis])])


def by_core(mine, got):
    first = lax.axis_index("c") == 0
    return jnp.stack([jnp.where(first, mine, got), jnp.where(first, got, mine)])


def halves(value, part):
    first = lax.axis_index("c") == 0
    low, high = value[..., :part], value[..., part:]
    return jnp.where(first, low, high), jnp.where(first, high, low)


def gather_plane(blocks):
    first = lax.axis_index("c") == 0
    keep = jnp.where(first, blocks[0], blocks[1])
    got = partner(jnp.where(first, blocks[1], blocks[0]), "c", 1)
    pair = by_core(keep, got)
    four = jnp.stack([pair] + [partner(pair, "y", k) for k in range(1, SIZE["y"])])
    return jnp.take(four, other_y(), axis=0, mode="clip")


def other_y():
    return jnp.arange(SIZE["y"], dtype=jnp.int32) ^ lax.axis_index("y")


def on_every(value, axis):
    spread = jnp.broadcast_to(value[None], (SIZE[axis],) + value.shape)
    return lax.all_to_all(spread, axis, split_axis=0, concat_axis=0, tiled=True)


def on_device(
    query_rows,
    corpus_rows,
    passage_length,
    candidate_owner,
    candidate_slot,
    norm_gain,
    project_weight,
    output_weight,
):
    bf16, f32, i32 = jnp.bfloat16, jnp.float32, jnp.int32
    cores, lines = SIZE["c"], SIZE["y"]
    plane = lines * cores
    tensors = SIZE["h"] * SIZE["x"]
    stored, passage_rows, features = corpus_rows.shape
    part = features // 2
    query_len = query_rows.shape[1]
    pairs = candidate_owner.shape[1]
    live = query_len + pairs * passage_rows
    rows = (live // ROW_TILE + 1) * ROW_TILE
    depth = project_weight.shape[0]
    options = pltpu.CompilerParams(vmem_limit_bytes=6 * MIB)

    raw = jnp.concatenate([corpus_rows.reshape(-1, features), query_rows[0]], axis=0)
    keep, give = halves(raw, part)
    shared = by_core(keep, partner(give, "c", 1))
    held = shared[:, : stored * passage_rows].reshape(2 * stored, passage_rows, part)
    queries = shared[:, stored * passage_rows :]
    output_weight, project_weight, held = lax.optimization_barrier(
        (output_weight, project_weight, held)
    )
    library = lax.all_gather(held, "z", axis=0, tiled=True)

    cells = [(z, q, t) for z in range(SIZE["z"]) for q in range(plane) for t in range(tensors)]
    number = {cell: i for i, cell in enumerate(cells)}
    turn = [(number[(z, q, t)], number[(t, q, z)]) for z, q, t in cells]
    narrow = lax.ppermute(output_weight.T, AXES, turn)
    narrow = narrow.reshape(depth, 2, HEAD_DIM).transpose(1, 0, 2)
    wide = project_weight.reshape(depth, 3, 2, HEAD_DIM).transpose(2, 0, 1, 3)
    wide = wide.reshape(2, depth, 3 * HEAD_DIM)
    asked = jnp.concatenate([candidate_owner, candidate_slot], axis=1).astype(bf16)
    asked = jnp.pad(asked, ((0, 7), (0, 4 * HEAD_DIM - 2 * pairs)))
    weight = jnp.concatenate([wide, narrow], axis=2)
    weight = jnp.concatenate([weight, jnp.broadcast_to(asked, (2,) + asked.shape)], axis=1)
    weight = gather_plane(weight)
    asked = weight[:, :, depth, : 2 * pairs].astype(i32)
    weight = weight[:, :, :depth].reshape(plane * depth, 4 * HEAD_DIM)
    weight = lax.all_gather(weight, "z", axis=0, tiled=True)

    owner, place = asked[:, :, :pairs], asked[:, :, pairs:]
    owner_z, owner_y, owner_c = owner // plane, owner // cores % lines, owner % cores
    wanted = (owner_z * cores + owner_c) * stored + place
    wanted = jnp.take(wanted, other_y(), axis=0, mode="clip").reshape(-1)
    block = jax.ShapeDtypeStruct((cores * pairs, passage_rows, part), bf16)
    outgoing = pl.pallas_call(
        pick_kernel,
        out_shape=[block] * lines,
        in_specs=[SMEM, VMEM],
        out_specs=[VMEM] * lines,
        compiler_params=options,
        name="pick",
    )(wanted, library)
    arrived = [outgoing[0]] + [partner(outgoing[k], "y", k) for k in range(1, lines)]

    here = lax.axis_index("y")
    source = lax.dynamic_index_in_dim(owner_y, here, axis=0, keepdims=False) ^ here
    stored_at = lax.dynamic_index_in_dim(owner * stored + place, here, axis=0, keepdims=False)
    counts = jnp.take(passage_length, stored_at.reshape(-1), axis=0, mode="clip")
    gain, _ = halves(norm_gain[None], part)
    packed = pl.pallas_call(
        pack_kernel,
        out_shape=jax.ShapeDtypeStruct((cores, rows, part), bf16),
        in_specs=[SMEM] * 2 + [VMEM] * (lines + 2),
        out_specs=VMEM,
        compiler_params=options,
        name="pack",
    )(source.reshape(-1), counts, *arrived, queries, gain)

    own_full = on_every(packed, "x")
    far_full = on_every(partner(packed, "h", 1), "x")
    own_swap = partner(own_full, "c", 1)
    far_swap = partner(far_full, "c", 1)
    far_swap, weight = lax.optimization_barrier((far_swap, weight))

    row = np.arange(rows)
    slot = np.where(row < query_len, row, query_len + (row - query_len) % passage_rows)
    half = HEAD_DIM // 2
    frequency = np.power(10000.0, -2.0 * np.arange(half) / HEAD_DIM).astype(np.float32)
    angles = slot.astype(np.float32)[:, None] * frequency[None, :]
    cosine, sine = np.cos(angles), np.sin(angles)
    normed = pl.pallas_call(
        functools.partial(norm_kernel, gain_row=live),
        out_shape=jax.ShapeDtypeStruct((cores * rows, tensors * features), bf16),
        in_specs=[VMEM] * 4,
        out_specs=VMEM,
        compiler_params=pltpu.CompilerParams(vmem_limit_bytes=16 * MIB),
        cost_estimate=pl.CostEstimate(
            flops=8 * rows * tensors * features,
            bytes_accessed=8 * MIB,
            transcendentals=2 * rows,
        ),
        name="norm",
    )(own_full, far_full, own_swap, far_swap)
    attended, spread = pl.pallas_call(
        functools.partial(attention_kernel, query_len=query_len, passage_rows=passage_rows),
        out_shape=[
            jax.ShapeDtypeStruct((cores, rows, HEAD_DIM), bf16),
            jax.ShapeDtypeStruct((cores, SIZE["x"], rows, HEAD_DIM), bf16),
        ],
        in_specs=[SMEM] + [VMEM] * 4,
        out_specs=[VMEM] * 2,
        compiler_params=pltpu.CompilerParams(vmem_limit_bytes=16 * MIB),
        cost_estimate=pl.CostEstimate(
            flops=2 * rows * tensors * features * 6 * HEAD_DIM,
            bytes_accessed=8 * MIB,
            transcendentals=2 * rows * rows,
        ),
        name="attention",
    )(
        counts,
        normed,
        weight,
        jnp.asarray(np.concatenate([cosine, cosine], axis=1), f32),
        jnp.asarray(np.concatenate([-sine, sine], axis=1), f32),
    )

    far = partner(attended, "h", 1)
    own_heads = lax.all_to_all(
        spread.reshape(-1, rows, HEAD_DIM), ("c", "x"), split_axis=0, concat_axis=0, tiled=True
    )
    far = jnp.broadcast_to(far[:, None], spread.shape).reshape(own_heads.shape)
    far_heads = lax.all_to_all(far, ("c", "x"), split_axis=0, concat_axis=0, tiled=True)
    own_out = weight[:, 3 * HEAD_DIM :]
    own_out, _ = lax.optimization_barrier((own_out, attended))
    other_out = partner(own_out, "c", 1)
    core = lax.axis_index("c")
    near_rows = lax.dynamic_index_in_dim(packed, core, axis=0, keepdims=False)
    far_rows = lax.dynamic_slice(
        own_swap, (lax.axis_index("x"), core, 0, 0), (1, 1, rows, part)
    ).reshape(rows, part)
    return pl.pallas_call(
        functools.partial(
            output_kernel, query_len=query_len, pairs=pairs, passage_rows=passage_rows
        ),
        out_shape=jax.ShapeDtypeStruct((pairs * (query_len + passage_rows), features), bf16),
        in_specs=[VMEM] * 6,
        out_specs=VMEM,
        compiler_params=options,
        cost_estimate=pl.CostEstimate(
            flops=2 * rows * tensors * 2 * HEAD_DIM * features,
            bytes_accessed=3 * 1024 * 1024,
            transcendentals=0,
        ),
        name="output",
    )(own_heads, far_heads, own_out, other_out, near_rows, far_rows)


def solution(mesh):
    fine = Mesh(mesh.devices.reshape([size for _, size in SPLIT]), AXES)
    placed = (
        P(CORPUS, None, TENSOR),
        P(CORPUS, None, TENSOR),
        P(),
        P(CORPUS, None),
        P(CORPUS, None),
        P(TENSOR),
        P(CORPUS, None, TENSOR),
        P(TENSOR, CORPUS),
    )
    return jax.shard_map(
        on_device, mesh=fine, in_specs=placed, out_specs=P(CORPUS, TENSOR), check_vma=False
    )
```

```python
import functools

import jax
import jax.numpy as jnp
import numpy as np
from jax import lax
from jax.experimental import pallas as pl
from jax.experimental.pallas import tpu as pltpu
from jax.sharding import Mesh, PartitionSpec as P

HEAD_DIM = 128
ROW_TILE = 16
SPLIT = (("z", 8), ("y", 4), ("c", 2), ("h", 2), ("x", 4))
SIZE = dict(SPLIT)
AXES = tuple(name for name, _ in SPLIT)
CORPUS = ("z", "y", "c")
TENSOR = ("h", "x")
VMEM = pl.BlockSpec(memory_space=pltpu.VMEM)
SMEM = pl.BlockSpec(memory_space=pltpu.SMEM)
MIB = 1024 * 1024


def pick_kernel(index_ref, library_ref, *out_refs):
    count = out_refs[0].shape[0]
    for block, out_ref in enumerate(out_refs):
        for i in range(count):
            out_ref[i] = library_ref[index_ref[block * count + i]]


def pack_kernel(source_ref, count_ref, *refs):
    f32 = jnp.float32
    part_refs, (query_ref, gain_ref, packed_ref) = refs[:-3], refs[-3:]
    groups, rows, part = packed_ref.shape
    passage_rows = part_refs[0].shape[1]
    pairs = part_refs[0].shape[0] // groups
    place = lax.broadcasted_iota(jnp.int32, (passage_rows, part), 0)
    for group in range(groups):
        blocks = [query_ref[group].astype(f32)]
        for pair in range(pairs):
            spot = group * pairs + pair
            source = source_ref[spot]
            passage = part_refs[0][spot].astype(f32)
            for k in range(1, len(part_refs)):
                passage = jnp.where(source == k, part_refs[k][spot].astype(f32), passage)
            blocks.append(jnp.where(place < count_ref[spot], passage, 0.0))
        filled = blocks[0].shape[0] + pairs * passage_rows
        blocks.append(jnp.broadcast_to(gain_ref[...].astype(f32), (rows - filled, part)))
        packed_ref[group] = jnp.concatenate(blocks, axis=0).astype(packed_ref.dtype)


def spread_kernel(packed_ref, spread_ref):
    for x in range(spread_ref.shape[0]):
        spread_ref[x] = packed_ref[...]


def attention_kernel(
    count_ref, own_ref, far_ref, own_swap_ref, far_swap_ref, weight_ref, cos_ref, sin_ref,
    out_ref, normed_ref, *, query_len, passage_rows,
):
    bf16, f32, i32 = jnp.bfloat16, jnp.float32, jnp.int32
    spread, groups, rows, part = own_ref.shape
    width = 4 * spread * part
    pairs = count_ref.shape[0] // groups
    gain_row = query_len + pairs * passage_rows
    core, high = lax.axis_index("c"), lax.axis_index("h")
    quarters = (
        (own_ref, high, core),
        (far_ref, 1 - high, core),
        (own_swap_ref, high, 1 - core),
        (far_swap_ref, 1 - high, 1 - core),
    )
    for group in range(groups):
        total = jnp.zeros((rows, HEAD_DIM), f32)
        for ref, _, _ in quarters:
            for x in range(spread):
                chunk = ref[x, group].astype(f32)
                square = chunk * chunk
                for lane in range(0, part, HEAD_DIM):
                    total = total + square[:, lane : lane + HEAD_DIM]
        inverse = lax.rsqrt(jnp.sum(total, axis=1, keepdims=True) / width + 1e-05)
        for ref, upper, half in quarters:
            for x in range(spread):
                chunk = ref[x, group].astype(f32)
                gain = chunk[gain_row : gain_row + 1, :]
                begin = pl.multiple_of(((upper * spread + x) * 2 + half) * part, part)
                normed_ref[group * rows : (group + 1) * rows, pl.ds(begin, part)] = (
                    chunk * inverse * gain
                ).astype(bf16)
    projected = jnp.dot(
        normed_ref[...], weight_ref[...], preferred_element_type=f32
    )

    def rotate(inputs):
        return (
            inputs * cos_ref[...] + pltpu.roll(inputs, HEAD_DIM // 2, 1) * sin_ref[...]
        ).astype(bf16)

    def pair_of(row):
        pair = jnp.full(row.shape, -1, i32)
        for k in range(pairs + 1):
            pair = jnp.where(row >= query_len + k * passage_rows, k, pair)
        return pair

    query_row = lax.broadcasted_iota(i32, (rows, 1), 0)
    key_row = lax.broadcasted_iota(i32, (1, rows), 1)
    query_pair, key_pair = pair_of(query_row), pair_of(key_row)
    for group in range(groups):
        end = jnp.full((1, rows), query_len, i32)
        for k in range(pairs):
            last = query_len + k * passage_rows + count_ref[group * pairs + k]
            end = jnp.where(key_pair == k, last, end)
        key_live = jnp.where(key_row < end, key_pair, -2)
        allowed = (key_row <= query_row) & ((key_live == -1) | (key_live == query_pair))
        mine = projected[group * rows : (group + 1) * rows]
        queries = rotate(mine[:, :HEAD_DIM])
        keys = rotate(mine[:, HEAD_DIM : 2 * HEAD_DIM])
        values = mine[:, 2 * HEAD_DIM :].astype(bf16)
        scores = lax.dot_general(
            queries, keys, (((1,), (1,)), ((), ())), preferred_element_type=f32
        ) * (1.0 / float(HEAD_DIM) ** 0.5)
        scores = jnp.where(allowed, scores, -1e30)
        exponent = jnp.exp(scores - jnp.max(scores, axis=-1, keepdims=True))
        weights = (exponent / jnp.sum(exponent, axis=-1, keepdims=True)).astype(bf16)
        attended = jnp.dot(weights, values, preferred_element_type=f32).astype(bf16)
        for t in range(out_ref.shape[1]):
            out_ref[group, t] = attended


def output_kernel(heads_ref, own_ref, other_ref, near_ref, far_ref, out_ref, *, query_len, pairs, passage_rows):
    bf16, f32 = jnp.bfloat16, jnp.float32
    core = lax.axis_index("c")
    numbers = (((1,), (1,)), ((), ()))
    tensors = heads_ref.shape[0] // 2
    columns = own_ref.shape[0] // tensors
    near, far = near_ref[...], far_ref[...]
    first = core == 0
    final = jnp.concatenate(
        [jnp.where(first, near, far), jnp.where(first, far, near)], axis=1
    ).astype(f32)
    summed = jnp.zeros(final.shape, f32)
    for t in range(tensors):
        block = slice(t * columns, (t + 1) * columns)
        partial_value = lax.dot_general(
            heads_ref[core * tensors + t], own_ref[block], numbers, preferred_element_type=f32
        ) + lax.dot_general(
            heads_ref[(1 - core) * tensors + t], other_ref[block], numbers, preferred_element_type=f32
        )
        summed = summed + partial_value.astype(bf16).astype(f32)
    final = final + summed
    blocks = []
    for pair in range(pairs):
        begin = query_len + pair * passage_rows
        blocks += [final[:query_len], final[begin : begin + passage_rows]]
    out_ref[...] = jnp.concatenate(blocks, axis=0).astype(bf16)


def partner(value, axis, bit):
    return lax.ppermute(value, axis, [(i, i ^ bit) for i in range(SIZE[axis])])


def by_core(mine, got):
    first = lax.axis_index("c") == 0
    return jnp.stack([jnp.where(first, mine, got), jnp.where(first, got, mine)])


def halves(value, part):
    first = lax.axis_index("c") == 0
    low, high = value[..., :part], value[..., part:]
    return jnp.where(first, low, high), jnp.where(first, high, low)


def gather_plane(blocks):
    first = lax.axis_index("c") == 0
    keep = jnp.where(first, blocks[0], blocks[1])
    got = partner(jnp.where(first, blocks[1], blocks[0]), "c", 1)
    pair = by_core(keep, got)
    four = jnp.stack([pair] + [partner(pair, "y", k) for k in range(1, SIZE["y"])])
    return jnp.take(four, other_y(), axis=0, mode="clip")


def other_y():
    return jnp.arange(SIZE["y"], dtype=jnp.int32) ^ lax.axis_index("y")


def on_every(value, axis):
    spread = jnp.broadcast_to(value[None], (SIZE[axis],) + value.shape)
    return lax.all_to_all(spread, axis, split_axis=0, concat_axis=0, tiled=True)


def on_device(
    query_rows,
    corpus_rows,
    passage_length,
    candidate_owner,
    candidate_slot,
    norm_gain,
    project_weight,
    output_weight,
):
    bf16, f32, i32 = jnp.bfloat16, jnp.float32, jnp.int32
    cores, lines = SIZE["c"], SIZE["y"]
    plane = lines * cores
    tensors = SIZE["h"] * SIZE["x"]
    stored, passage_rows, features = corpus_rows.shape
    part = features // 2
    query_len = query_rows.shape[1]
    pairs = candidate_owner.shape[1]
    live = query_len + pairs * passage_rows
    rows = (live // ROW_TILE + 1) * ROW_TILE
    depth = project_weight.shape[0]
    options = pltpu.CompilerParams(vmem_limit_bytes=6 * MIB)

    raw = jnp.concatenate([corpus_rows.reshape(-1, features), query_rows[0]], axis=0)
    keep, give = halves(raw, part)
    shared = by_core(keep, partner(give, "c", 1))
    held = shared[:, : stored * passage_rows].reshape(2 * stored, passage_rows, part)
    queries = shared[:, stored * passage_rows :]
    output_weight, project_weight, held = lax.optimization_barrier(
        (output_weight, project_weight, held)
    )
    library = lax.all_gather(held, "z", axis=0, tiled=True)

    cells = [(z, q, t) for z in range(SIZE["z"]) for q in range(plane) for t in range(tensors)]
    number = {cell: i for i, cell in enumerate(cells)}
    turn = [(number[(z, q, t)], number[(t, q, z)]) for z, q, t in cells]
    narrow = lax.ppermute(output_weight.T, AXES, turn)
    narrow = narrow.reshape(depth, 2, HEAD_DIM).transpose(1, 0, 2)
    wide = project_weight.reshape(depth, 3, 2, HEAD_DIM).transpose(2, 0, 1, 3)
    wide = wide.reshape(2, depth, 3 * HEAD_DIM)
    asked = jnp.concatenate([candidate_owner, candidate_slot], axis=1).astype(bf16)
    asked = jnp.pad(asked, ((0, 7), (0, 4 * HEAD_DIM - 2 * pairs)))
    weight = jnp.concatenate([wide, narrow], axis=2)
    weight = jnp.concatenate([weight, jnp.broadcast_to(asked, (2,) + asked.shape)], axis=1)
    weight = gather_plane(weight)
    asked = weight[:, :, depth, : 2 * pairs].astype(i32)
    weight = weight[:, :, :depth].reshape(plane * depth, 4 * HEAD_DIM)
    own_out = lax.all_gather(weight[:, 3 * HEAD_DIM :], "z", axis=0, tiled=True)
    weight = lax.all_gather(weight[:, : 3 * HEAD_DIM], "z", axis=0, tiled=True)

    owner, place = asked[:, :, :pairs], asked[:, :, pairs:]
    owner_z, owner_y, owner_c = owner // plane, owner // cores % lines, owner % cores
    wanted = (owner_z * cores + owner_c) * stored + place
    wanted = jnp.take(wanted, other_y(), axis=0, mode="clip").reshape(-1)
    block = jax.ShapeDtypeStruct((cores * pairs, passage_rows, part), bf16)
    outgoing = pl.pallas_call(
        pick_kernel,
        out_shape=[block] * lines,
        in_specs=[SMEM, VMEM],
        out_specs=[VMEM] * lines,
        compiler_params=options,
        name="pick",
    )(wanted, library)
    arrived = [outgoing[0]] + [partner(outgoing[k], "y", k) for k in range(1, lines)]

    here = lax.axis_index("y")
    source = lax.dynamic_index_in_dim(owner_y, here, axis=0, keepdims=False) ^ here
    stored_at = lax.dynamic_index_in_dim(owner * stored + place, here, axis=0, keepdims=False)
    counts = jnp.take(passage_length, stored_at.reshape(-1), axis=0, mode="clip")
    gain, _ = halves(norm_gain[None], part)
    packed = pl.pallas_call(
        pack_kernel,
        out_shape=jax.ShapeDtypeStruct((cores, rows, part), bf16),
        in_specs=[SMEM] * 2 + [VMEM] * (lines + 2),
        out_specs=VMEM,
        compiler_params=options,
        name="pack",
    )(source.reshape(-1), counts, *arrived, queries, gain)

    far = partner(packed, "h", 1)
    own_full = on_every(packed, "x")
    far = pl.pallas_call(
        spread_kernel,
        out_shape=jax.ShapeDtypeStruct((SIZE["x"],) + packed.shape, bf16),
        in_specs=[VMEM],
        out_specs=VMEM,
        compiler_params=options,
        cost_estimate=pl.CostEstimate(flops=0, bytes_accessed=4 * MIB, transcendentals=0),
        name="spread",
    )(far)
    far_full = lax.all_to_all(far, "x", split_axis=0, concat_axis=0, tiled=True)
    own_swap = partner(own_full, "c", 1)
    far_full, weight = lax.optimization_barrier((far_full, weight))
    far_swap = partner(far_full, "c", 1)

    row = np.arange(rows)
    slot = np.where(row < query_len, row, query_len + (row - query_len) % passage_rows)
    half = HEAD_DIM // 2
    frequency = np.power(10000.0, -2.0 * np.arange(half) / HEAD_DIM).astype(np.float32)
    angles = slot.astype(np.float32)[:, None] * frequency[None, :]
    cosine, sine = np.cos(angles), np.sin(angles)
    attended = pl.pallas_call(
        functools.partial(attention_kernel, query_len=query_len, passage_rows=passage_rows),
        out_shape=jax.ShapeDtypeStruct((cores, tensors, rows, HEAD_DIM), bf16),
        in_specs=[SMEM] + [VMEM] * 7,
        out_specs=VMEM,
        scratch_shapes=[pltpu.VMEM((cores * rows, tensors * features), bf16)],
        compiler_params=pltpu.CompilerParams(vmem_limit_bytes=18 * MIB),
        cost_estimate=pl.CostEstimate(
            flops=2 * rows * tensors * features * 6 * HEAD_DIM,
            bytes_accessed=8 * 1024 * 1024,
            transcendentals=2 * rows * rows,
        ),
        name="attention",
    )(
        counts,
        own_full,
        far_full,
        own_swap,
        far_swap,
        weight,
        jnp.asarray(np.concatenate([cosine, cosine], axis=1), f32),
        jnp.asarray(np.concatenate([-sine, sine], axis=1), f32),
    )

    heads = lax.all_to_all(
        attended.reshape(-1, rows, HEAD_DIM),
        ("c",) + TENSOR,
        split_axis=0,
        concat_axis=0,
        tiled=True,
    )
    own_out, _ = lax.optimization_barrier((own_out, attended))
    core = lax.axis_index("c")
    near_rows = lax.dynamic_index_in_dim(packed, core, axis=0, keepdims=False)
    far_rows = lax.dynamic_slice(
        own_swap, (lax.axis_index("x"), core, 0, 0), (1, 1, rows, part)
    ).reshape(rows, part)
    other_out = partner(own_out, "c", 1)
    return pl.pallas_call(
        functools.partial(
            output_kernel, query_len=query_len, pairs=pairs, passage_rows=passage_rows
        ),
        out_shape=jax.ShapeDtypeStruct((pairs * (query_len + passage_rows), features), bf16),
        in_specs=[VMEM] * 5,
        out_specs=VMEM,
        compiler_params=options,
        cost_estimate=pl.CostEstimate(
            flops=2 * rows * tensors * 2 * HEAD_DIM * features,
            bytes_accessed=3 * 1024 * 1024,
            transcendentals=0,
        ),
        name="output",
    )(heads, own_out, other_out, near_rows, far_rows)


def solution(mesh):
    fine = Mesh(mesh.devices.reshape([size for _, size in SPLIT]), AXES)
    placed = (
        P(CORPUS, None, TENSOR),
        P(CORPUS, None, TENSOR),
        P(),
        P(CORPUS, None),
        P(CORPUS, None),
        P(TENSOR),
        P(CORPUS, None, TENSOR),
        P(TENSOR, CORPUS),
    )
    return jax.shard_map(
        on_device, mesh=fine, in_specs=placed, out_specs=P(CORPUS, TENSOR), check_vma=False
    )
```

```python
import functools

import jax
import jax.numpy as jnp
import numpy as np
from jax import lax
from jax.experimental import pallas as pl
from jax.experimental.pallas import tpu as pltpu
from jax.sharding import Mesh, PartitionSpec as P

HEAD_DIM = 128
ROW_TILE = 16
SPLIT = (("zr", 4), ("zb", 2), ("y", 4), ("c", 2), ("h", 2), ("x", 4))
SIZE = dict(SPLIT)
AXES = tuple(name for name, _ in SPLIT)
Z = ("zr", "zb")
CORPUS = Z + ("y", "c")
TENSOR = ("h", "x")
VMEM = pl.BlockSpec(memory_space=pltpu.VMEM)
SMEM = pl.BlockSpec(memory_space=pltpu.SMEM)
MIB = 1024 * 1024


def pick_kernel(index_ref, library_ref, *out_refs):
    count = out_refs[0].shape[0]
    for block, out_ref in enumerate(out_refs):
        for i in range(count):
            out_ref[i] = library_ref[index_ref[block * count + i]]


def pack_kernel(source_ref, count_ref, *refs):
    f32 = jnp.float32
    part_refs, (query_ref, gain_ref, packed_ref) = refs[:-3], refs[-3:]
    groups, rows, part = packed_ref.shape
    passage_rows = part_refs[0].shape[1]
    pairs = part_refs[0].shape[0] // groups
    place = lax.broadcasted_iota(jnp.int32, (passage_rows, part), 0)
    for group in range(groups):
        blocks = [query_ref[group].astype(f32)]
        for pair in range(pairs):
            spot = group * pairs + pair
            source = source_ref[spot]
            passage = part_refs[0][spot].astype(f32)
            for k in range(1, len(part_refs)):
                passage = jnp.where(source == k, part_refs[k][spot].astype(f32), passage)
            blocks.append(jnp.where(place < count_ref[spot], passage, 0.0))
        filled = blocks[0].shape[0] + pairs * passage_rows
        blocks.append(jnp.broadcast_to(gain_ref[...].astype(f32), (rows - filled, part)))
        packed_ref[group] = jnp.concatenate(blocks, axis=0).astype(packed_ref.dtype)


def spread_kernel(packed_ref, spread_ref):
    for x in range(spread_ref.shape[0]):
        spread_ref[x] = packed_ref[...]


def attention_kernel(
    count_ref, own_ref, far_ref, own_swap_ref, far_swap_ref, weight_ref, cos_ref, sin_ref,
    out_ref, normed_ref, *, query_len, passage_rows,
):
    bf16, f32, i32 = jnp.bfloat16, jnp.float32, jnp.int32
    spread, groups, rows, part = own_ref.shape
    width = 4 * spread * part
    pairs = count_ref.shape[0] // groups
    gain_row = query_len + pairs * passage_rows
    core, high = lax.axis_index("c"), lax.axis_index("h")
    quarters = (
        (own_ref, high, core),
        (far_ref, 1 - high, core),
        (own_swap_ref, high, 1 - core),
        (far_swap_ref, 1 - high, 1 - core),
    )
    for group in range(groups):
        total = jnp.zeros((rows, HEAD_DIM), f32)
        for ref, _, _ in quarters:
            for x in range(spread):
                chunk = ref[x, group].astype(f32)
                square = chunk * chunk
                for lane in range(0, part, HEAD_DIM):
                    total = total + square[:, lane : lane + HEAD_DIM]
        inverse = lax.rsqrt(jnp.sum(total, axis=1, keepdims=True) / width + 1e-05)
        for ref, upper, half in quarters:
            for x in range(spread):
                chunk = ref[x, group].astype(f32)
                gain = chunk[gain_row : gain_row + 1, :]
                begin = pl.multiple_of(((upper * spread + x) * 2 + half) * part, part)
                normed_ref[group * rows : (group + 1) * rows, pl.ds(begin, part)] = (
                    chunk * inverse * gain
                ).astype(bf16)
    projected = jnp.dot(
        normed_ref[...], weight_ref[...], preferred_element_type=f32
    )

    def rotate(inputs):
        return (
            inputs * cos_ref[...] + pltpu.roll(inputs, HEAD_DIM // 2, 1) * sin_ref[...]
        ).astype(bf16)

    def pair_of(row):
        pair = jnp.full(row.shape, -1, i32)
        for k in range(pairs + 1):
            pair = jnp.where(row >= query_len + k * passage_rows, k, pair)
        return pair

    query_row = lax.broadcasted_iota(i32, (rows, 1), 0)
    key_row = lax.broadcasted_iota(i32, (1, rows), 1)
    query_pair, key_pair = pair_of(query_row), pair_of(key_row)
    for group in range(groups):
        end = jnp.full((1, rows), query_len, i32)
        for k in range(pairs):
            last = query_len + k * passage_rows + count_ref[group * pairs + k]
            end = jnp.where(key_pair == k, last, end)
        key_live = jnp.where(key_row < end, key_pair, -2)
        allowed = (key_row <= query_row) & ((key_live == -1) | (key_live == query_pair))
        mine = projected[group * rows : (group + 1) * rows]
        queries = rotate(mine[:, :HEAD_DIM])
        keys = rotate(mine[:, HEAD_DIM : 2 * HEAD_DIM])
        values = mine[:, 2 * HEAD_DIM :].astype(bf16)
        scores = lax.dot_general(
            queries, keys, (((1,), (1,)), ((), ())), preferred_element_type=f32
        ) * (1.0 / float(HEAD_DIM) ** 0.5)
        scores = jnp.where(allowed, scores, -1e30)
        exponent = jnp.exp(scores - jnp.max(scores, axis=-1, keepdims=True))
        weights = (exponent / jnp.sum(exponent, axis=-1, keepdims=True)).astype(bf16)
        attended = jnp.dot(weights, values, preferred_element_type=f32).astype(bf16)
        for t in range(out_ref.shape[1]):
            out_ref[group, t] = attended


def output_kernel(heads_ref, own_ref, other_ref, near_ref, far_ref, out_ref, *, query_len, pairs, passage_rows):
    bf16, f32 = jnp.bfloat16, jnp.float32
    core = lax.axis_index("c")
    numbers = (((1,), (1,)), ((), ()))
    tensors = heads_ref.shape[0] // 2
    columns = own_ref.shape[0] // tensors
    near, far = near_ref[...], far_ref[...]
    first = core == 0
    final = jnp.concatenate(
        [jnp.where(first, near, far), jnp.where(first, far, near)], axis=1
    ).astype(f32)
    summed = jnp.zeros(final.shape, f32)
    for t in range(tensors):
        block = slice(t * columns, (t + 1) * columns)
        partial_value = lax.dot_general(
            heads_ref[core * tensors + t], own_ref[block], numbers, preferred_element_type=f32
        ) + lax.dot_general(
            heads_ref[(1 - core) * tensors + t], other_ref[block], numbers, preferred_element_type=f32
        )
        summed = summed + partial_value.astype(bf16).astype(f32)
    final = final + summed
    blocks = []
    for pair in range(pairs):
        begin = query_len + pair * passage_rows
        blocks += [final[:query_len], final[begin : begin + passage_rows]]
    out_ref[...] = jnp.concatenate(blocks, axis=0).astype(bf16)


def partner(value, axis, bit):
    return lax.ppermute(value, axis, [(i, i ^ bit) for i in range(SIZE[axis])])


def in_order(mine, got, axis):
    first = lax.axis_index(axis) == 0
    return jnp.stack([jnp.where(first, mine, got), jnp.where(first, got, mine)])


def halves(value, part):
    first = lax.axis_index("c") == 0
    low, high = value[..., :part], value[..., part:]
    return jnp.where(first, low, high), jnp.where(first, high, low)


def gather_plane(blocks):
    first = lax.axis_index("c") == 0
    keep = jnp.where(first, blocks[0], blocks[1])
    got = partner(jnp.where(first, blocks[1], blocks[0]), "c", 1)
    pair = in_order(keep, got, "c")
    four = jnp.stack([pair] + [partner(pair, "y", k) for k in range(1, SIZE["y"])])
    return jnp.take(four, other_y(), axis=0, mode="clip")


def other_y():
    return jnp.arange(SIZE["y"], dtype=jnp.int32) ^ lax.axis_index("y")


def on_every(value, axis):
    spread = jnp.broadcast_to(value[None], (SIZE[axis],) + value.shape)
    return lax.all_to_all(spread, axis, split_axis=0, concat_axis=0, tiled=True)


def on_device(
    query_rows,
    corpus_rows,
    passage_length,
    candidate_owner,
    candidate_slot,
    norm_gain,
    project_weight,
    output_weight,
):
    bf16, f32, i32 = jnp.bfloat16, jnp.float32, jnp.int32
    cores, lines = SIZE["c"], SIZE["y"]
    plane = lines * cores
    tensors = SIZE["h"] * SIZE["x"]
    stored, passage_rows, features = corpus_rows.shape
    part = features // 2
    query_len = query_rows.shape[1]
    pairs = candidate_owner.shape[1]
    live = query_len + pairs * passage_rows
    rows = (live // ROW_TILE + 1) * ROW_TILE
    depth = project_weight.shape[0]
    options = pltpu.CompilerParams(vmem_limit_bytes=6 * MIB)

    raw = jnp.concatenate([corpus_rows.reshape(-1, features), query_rows[0]], axis=0)
    keep, give = halves(raw, part)
    shared = in_order(keep, partner(give, "c", 1), "c")
    held = shared[:, : stored * passage_rows].reshape(2 * stored, passage_rows, part)
    queries = shared[:, stored * passage_rows :]
    output_weight, project_weight, held = lax.optimization_barrier(
        (output_weight, project_weight, held)
    )
    library = lax.all_gather(held, Z, axis=0, tiled=True)

    cells = [(z, q, t) for z in range(tensors) for q in range(plane) for t in range(tensors)]
    number = {cell: i for i, cell in enumerate(cells)}
    turn = [(number[(z, q, t)], number[(t, q, z)]) for z, q, t in cells]
    narrow = lax.ppermute(output_weight.T, AXES, turn)
    narrow = narrow.reshape(depth, 2, HEAD_DIM).transpose(1, 0, 2)
    wide = project_weight.reshape(depth, 3, 2, HEAD_DIM).transpose(2, 0, 1, 3)
    wide = wide.reshape(2, depth, 3 * HEAD_DIM)
    asked = jnp.concatenate([candidate_owner, candidate_slot], axis=1).astype(bf16)
    asked = jnp.pad(asked, ((0, 7), (0, 4 * HEAD_DIM - 2 * pairs)))
    weight = jnp.concatenate([wide, narrow], axis=2)
    weight = jnp.concatenate([weight, jnp.broadcast_to(asked, (2,) + asked.shape)], axis=1)
    weight = gather_plane(weight)
    asked = weight[:, :, depth, : 2 * pairs].astype(i32)
    weight = weight[:, :, :depth].reshape(plane * depth, 4 * HEAD_DIM)
    narrow = weight[:, 3 * HEAD_DIM :]
    narrow = in_order(narrow, partner(narrow, "zb", 1), "zb").reshape(-1, HEAD_DIM)
    narrow, asked = lax.optimization_barrier((narrow, asked))
    own_out = lax.all_gather(narrow, "zr", axis=0, tiled=True)
    weight = lax.all_gather(weight[:, : 3 * HEAD_DIM], Z, axis=0, tiled=True)

    owner, place = asked[:, :, :pairs], asked[:, :, pairs:]
    owner_z, owner_y, owner_c = owner // plane, owner // cores % lines, owner % cores
    wanted = (owner_z * cores + owner_c) * stored + place
    wanted = jnp.take(wanted, other_y(), axis=0, mode="clip").reshape(-1)
    block = jax.ShapeDtypeStruct((cores * pairs, passage_rows, part), bf16)
    outgoing = pl.pallas_call(
        pick_kernel,
        out_shape=[block] * lines,
        in_specs=[SMEM, VMEM],
        out_specs=[VMEM] * lines,
        compiler_params=options,
        name="pick",
    )(wanted, library)
    arrived = [outgoing[0]] + [partner(outgoing[k], "y", k) for k in range(1, lines)]

    here = lax.axis_index("y")
    source = lax.dynamic_index_in_dim(owner_y, here, axis=0, keepdims=False) ^ here
    stored_at = lax.dynamic_index_in_dim(owner * stored + place, here, axis=0, keepdims=False)
    counts = jnp.take(passage_length, stored_at.reshape(-1), axis=0, mode="clip")
    gain, _ = halves(norm_gain[None], part)
    packed = pl.pallas_call(
        pack_kernel,
        out_shape=jax.ShapeDtypeStruct((cores, rows, part), bf16),
        in_specs=[SMEM] * 2 + [VMEM] * (lines + 2),
        out_specs=VMEM,
        compiler_params=options,
        name="pack",
    )(source.reshape(-1), counts, *arrived, queries, gain)

    far = partner(packed, "h", 1)
    own_full = lax.all_gather(packed, "x", axis=0)
    far, own_full = lax.optimization_barrier((far, own_full))
    far = pl.pallas_call(
        spread_kernel,
        out_shape=jax.ShapeDtypeStruct((SIZE["x"],) + packed.shape, bf16),
        in_specs=[VMEM],
        out_specs=VMEM,
        compiler_params=options,
        cost_estimate=pl.CostEstimate(flops=0, bytes_accessed=4 * MIB, transcendentals=0),
        name="spread",
    )(far)
    far_full = lax.all_to_all(far, "x", split_axis=0, concat_axis=0, tiled=True)
    own_swap = partner(own_full, "c", 1)
    far_full, weight = lax.optimization_barrier((far_full, weight))
    far_swap = partner(far_full, "c", 1)

    row = np.arange(rows)
    slot = np.where(row < query_len, row, query_len + (row - query_len) % passage_rows)
    half = HEAD_DIM // 2
    frequency = np.power(10000.0, -2.0 * np.arange(half) / HEAD_DIM).astype(np.float32)
    angles = slot.astype(np.float32)[:, None] * frequency[None, :]
    cosine, sine = np.cos(angles), np.sin(angles)
    attended = pl.pallas_call(
        functools.partial(attention_kernel, query_len=query_len, passage_rows=passage_rows),
        out_shape=jax.ShapeDtypeStruct((cores, tensors, rows, HEAD_DIM), bf16),
        in_specs=[SMEM] + [VMEM] * 7,
        out_specs=VMEM,
        scratch_shapes=[pltpu.VMEM((cores * rows, tensors * features), bf16)],
        compiler_params=pltpu.CompilerParams(vmem_limit_bytes=18 * MIB),
        cost_estimate=pl.CostEstimate(
            flops=2 * rows * tensors * features * 6 * HEAD_DIM,
            bytes_accessed=8 * 1024 * 1024,
            transcendentals=2 * rows * rows,
        ),
        name="attention",
    )(
        counts,
        own_full,
        far_full,
        own_swap,
        far_swap,
        weight,
        jnp.asarray(np.concatenate([cosine, cosine], axis=1), f32),
        jnp.asarray(np.concatenate([-sine, sine], axis=1), f32),
    )

    heads = lax.all_to_all(
        attended.reshape(-1, rows, HEAD_DIM),
        ("c",) + TENSOR,
        split_axis=0,
        concat_axis=0,
        tiled=True,
    )
    own_out, _ = lax.optimization_barrier((own_out, attended))
    core = lax.axis_index("c")
    near_rows = lax.dynamic_index_in_dim(packed, core, axis=0, keepdims=False)
    far_rows = lax.dynamic_slice(
        own_swap, (lax.axis_index("x"), core, 0, 0), (1, 1, rows, part)
    ).reshape(rows, part)
    other_out = partner(own_out, "c", 1)
    return pl.pallas_call(
        functools.partial(
            output_kernel, query_len=query_len, pairs=pairs, passage_rows=passage_rows
        ),
        out_shape=jax.ShapeDtypeStruct((pairs * (query_len + passage_rows), features), bf16),
        in_specs=[VMEM] * 5,
        out_specs=VMEM,
        compiler_params=options,
        cost_estimate=pl.CostEstimate(
            flops=2 * rows * tensors * 2 * HEAD_DIM * features,
            bytes_accessed=3 * 1024 * 1024,
            transcendentals=0,
        ),
        name="output",
    )(heads, own_out, other_out, near_rows, far_rows)


def solution(mesh):
    fine = Mesh(mesh.devices.reshape([size for _, size in SPLIT]), AXES)
    placed = (
        P(CORPUS, None, TENSOR),
        P(CORPUS, None, TENSOR),
        P(),
        P(CORPUS, None),
        P(CORPUS, None),
        P(TENSOR),
        P(CORPUS, None, TENSOR),
        P(TENSOR, CORPUS),
    )
    return jax.shard_map(
        on_device, mesh=fine, in_specs=placed, out_specs=P(CORPUS, TENSOR), check_vma=False
    )
```

```python
import functools

import jax
import jax.numpy as jnp
import numpy as np
from jax import lax
from jax.experimental import pallas as pl
from jax.experimental.pallas import tpu as pltpu
from jax.sharding import Mesh, PartitionSpec as P

HEAD_DIM = 128
ROW_TILE = 16
SPLIT = (("z", 8), ("y", 4), ("c", 2), ("h", 2), ("x", 4))
SIZE = dict(SPLIT)
AXES = tuple(name for name, _ in SPLIT)
CORPUS = ("z", "y", "c")
TENSOR = ("h", "x")
VMEM = pl.BlockSpec(memory_space=pltpu.VMEM)
SMEM = pl.BlockSpec(memory_space=pltpu.SMEM)
MIB = 1024 * 1024


def pick_kernel(index_ref, library_ref, *out_refs):
    count = out_refs[0].shape[0]
    for block, out_ref in enumerate(out_refs):
        for i in range(count):
            out_ref[i] = library_ref[index_ref[block * count + i]]


def pack_kernel(source_ref, count_ref, *refs):
    f32 = jnp.float32
    part_refs, (query_ref, gain_ref, packed_ref) = refs[:-3], refs[-3:]
    groups, rows, part = packed_ref.shape
    passage_rows = part_refs[0].shape[1]
    pairs = part_refs[0].shape[0] // groups
    place = lax.broadcasted_iota(jnp.int32, (passage_rows, part), 0)
    for group in range(groups):
        blocks = [query_ref[group].astype(f32)]
        for pair in range(pairs):
            spot = group * pairs + pair
            source = source_ref[spot]
            passage = part_refs[0][spot].astype(f32)
            for k in range(1, len(part_refs)):
                passage = jnp.where(source == k, part_refs[k][spot].astype(f32), passage)
            blocks.append(jnp.where(place < count_ref[spot], passage, 0.0))
        filled = blocks[0].shape[0] + pairs * passage_rows
        blocks.append(jnp.broadcast_to(gain_ref[...].astype(f32), (rows - filled, part)))
        packed_ref[group] = jnp.concatenate(blocks, axis=0).astype(packed_ref.dtype)


def spread_kernel(packed_ref, spread_ref):
    for x in range(spread_ref.shape[0]):
        spread_ref[x] = packed_ref[...]


def attention_kernel(
    count_ref, own_ref, far_ref, own_swap_ref, far_swap_ref, weight_ref, cos_ref, sin_ref,
    out_ref, own_out_ref, normed_ref, *, query_len, passage_rows,
):
    bf16, f32, i32 = jnp.bfloat16, jnp.float32, jnp.int32
    spread, groups, rows, part = own_ref.shape
    width = 4 * spread * part
    pairs = count_ref.shape[0] // groups
    gain_row = query_len + pairs * passage_rows
    core, high = lax.axis_index("c"), lax.axis_index("h")
    quarters = (
        (own_ref, high, core),
        (far_ref, 1 - high, core),
        (own_swap_ref, high, 1 - core),
        (far_swap_ref, 1 - high, 1 - core),
    )
    for group in range(groups):
        total = jnp.zeros((rows, HEAD_DIM), f32)
        for ref, _, _ in quarters:
            for x in range(spread):
                chunk = ref[x, group].astype(f32)
                square = chunk * chunk
                for lane in range(0, part, HEAD_DIM):
                    total = total + square[:, lane : lane + HEAD_DIM]
        inverse = lax.rsqrt(jnp.sum(total, axis=1, keepdims=True) / width + 1e-05)
        for ref, upper, half in quarters:
            for x in range(spread):
                chunk = ref[x, group].astype(f32)
                gain = chunk[gain_row : gain_row + 1, :]
                begin = pl.multiple_of(((upper * spread + x) * 2 + half) * part, part)
                normed_ref[group * rows : (group + 1) * rows, pl.ds(begin, part)] = (
                    chunk * inverse * gain
                ).astype(bf16)
    projected = jnp.dot(
        normed_ref[...], weight_ref[:, : 3 * HEAD_DIM], preferred_element_type=f32
    )

    own_out_ref[...] = weight_ref[:, 3 * HEAD_DIM :]

    def rotate(inputs):
        return (
            inputs * cos_ref[...] + pltpu.roll(inputs, HEAD_DIM // 2, 1) * sin_ref[...]
        ).astype(bf16)

    def pair_of(row):
        pair = jnp.full(row.shape, -1, i32)
        for k in range(pairs + 1):
            pair = jnp.where(row >= query_len + k * passage_rows, k, pair)
        return pair

    query_row = lax.broadcasted_iota(i32, (rows, 1), 0)
    key_row = lax.broadcasted_iota(i32, (1, rows), 1)
    query_pair, key_pair = pair_of(query_row), pair_of(key_row)
    for group in range(groups):
        end = jnp.full((1, rows), query_len, i32)
        for k in range(pairs):
            last = query_len + k * passage_rows + count_ref[group * pairs + k]
            end = jnp.where(key_pair == k, last, end)
        key_live = jnp.where(key_row < end, key_pair, -2)
        allowed = (key_row <= query_row) & ((key_live == -1) | (key_live == query_pair))
        mine = projected[group * rows : (group + 1) * rows]
        queries = rotate(mine[:, :HEAD_DIM])
        keys = rotate(mine[:, HEAD_DIM : 2 * HEAD_DIM])
        values = mine[:, 2 * HEAD_DIM :].astype(bf16)
        scores = lax.dot_general(
            queries, keys, (((1,), (1,)), ((), ())), preferred_element_type=f32
        ) * (1.0 / float(HEAD_DIM) ** 0.5)
        scores = jnp.where(allowed, scores, -1e30)
        exponent = jnp.exp(scores - jnp.max(scores, axis=-1, keepdims=True))
        weights = (exponent / jnp.sum(exponent, axis=-1, keepdims=True)).astype(bf16)
        attended = jnp.dot(weights, values, preferred_element_type=f32).astype(bf16)
        out_ref[group] = attended


def heads_kernel(own_ref, far_ref, spread_ref):
    high = lax.axis_index("h")
    groups = own_ref.shape[0]
    spread = spread_ref.shape[0] // groups
    for group in range(groups):
        for x in range(spread):
            spread_ref[group * spread + x, high] = own_ref[group]
            spread_ref[group * spread + x, 1 - high] = far_ref[group]


def output_kernel(heads_ref, own_ref, other_ref, near_ref, far_ref, out_ref, *, query_len, pairs, passage_rows):
    bf16, f32 = jnp.bfloat16, jnp.float32
    core = lax.axis_index("c")
    numbers = (((1,), (1,)), ((), ()))
    spread, highs = heads_ref.shape[0] // 2, heads_ref.shape[1]
    columns = own_ref.shape[0] // (spread * highs)
    near, far = near_ref[...], far_ref[...]
    first = core == 0
    final = jnp.concatenate(
        [jnp.where(first, near, far), jnp.where(first, far, near)], axis=1
    ).astype(f32)
    summed = jnp.zeros(final.shape, f32)
    for t in range(spread * highs):
        block, high, x = slice(t * columns, (t + 1) * columns), t // spread, t % spread
        partial_value = lax.dot_general(
            heads_ref[core * spread + x, high], own_ref[block], numbers, preferred_element_type=f32
        ) + lax.dot_general(
            heads_ref[(1 - core) * spread + x, high], other_ref[block], numbers, preferred_element_type=f32
        )
        summed = summed + partial_value.astype(bf16).astype(f32)
    final = final + summed
    blocks = []
    for pair in range(pairs):
        begin = query_len + pair * passage_rows
        blocks += [final[:query_len], final[begin : begin + passage_rows]]
    out_ref[...] = jnp.concatenate(blocks, axis=0).astype(bf16)


def partner(value, axis, bit):
    return lax.ppermute(value, axis, [(i, i ^ bit) for i in range(SIZE[axis])])


def by_core(mine, got):
    first = lax.axis_index("c") == 0
    return jnp.stack([jnp.where(first, mine, got), jnp.where(first, got, mine)])


def halves(value, part):
    first = lax.axis_index("c") == 0
    low, high = value[..., :part], value[..., part:]
    return jnp.where(first, low, high), jnp.where(first, high, low)


def gather_plane(blocks):
    first = lax.axis_index("c") == 0
    keep = jnp.where(first, blocks[0], blocks[1])
    got = partner(jnp.where(first, blocks[1], blocks[0]), "c", 1)
    pair = by_core(keep, got)
    four = jnp.stack([pair] + [partner(pair, "y", k) for k in range(1, SIZE["y"])])
    return jnp.take(four, other_y(), axis=0, mode="clip")


def other_y():
    return jnp.arange(SIZE["y"], dtype=jnp.int32) ^ lax.axis_index("y")


def on_every(value, axis):
    spread = jnp.broadcast_to(value[None], (SIZE[axis],) + value.shape)
    return lax.all_to_all(spread, axis, split_axis=0, concat_axis=0, tiled=True)


def on_device(
    query_rows,
    corpus_rows,
    passage_length,
    candidate_owner,
    candidate_slot,
    norm_gain,
    project_weight,
    output_weight,
):
    bf16, f32, i32 = jnp.bfloat16, jnp.float32, jnp.int32
    cores, lines = SIZE["c"], SIZE["y"]
    plane = lines * cores
    tensors = SIZE["h"] * SIZE["x"]
    stored, passage_rows, features = corpus_rows.shape
    part = features // 2
    query_len = query_rows.shape[1]
    pairs = candidate_owner.shape[1]
    live = query_len + pairs * passage_rows
    rows = (live // ROW_TILE + 1) * ROW_TILE
    depth = project_weight.shape[0]
    options = pltpu.CompilerParams(vmem_limit_bytes=6 * MIB)

    raw = jnp.concatenate([corpus_rows.reshape(-1, features), query_rows[0]], axis=0)
    keep, give = halves(raw, part)
    shared = by_core(keep, partner(give, "c", 1))
    held = shared[:, : stored * passage_rows].reshape(2 * stored, passage_rows, part)
    queries = shared[:, stored * passage_rows :]
    output_weight, project_weight, held = lax.optimization_barrier(
        (output_weight, project_weight, held)
    )
    library = lax.all_gather(held, "z", axis=0, tiled=True)

    cells = [(z, q, t) for z in range(SIZE["z"]) for q in range(plane) for t in range(tensors)]
    number = {cell: i for i, cell in enumerate(cells)}
    turn = [(number[(z, q, t)], number[(t, q, z)]) for z, q, t in cells]
    narrow = lax.ppermute(output_weight.T, AXES, turn)
    narrow = narrow.reshape(depth, 2, HEAD_DIM).transpose(1, 0, 2)
    wide = project_weight.reshape(depth, 3, 2, HEAD_DIM).transpose(2, 0, 1, 3)
    wide = wide.reshape(2, depth, 3 * HEAD_DIM)
    asked = jnp.concatenate([candidate_owner, candidate_slot], axis=1).astype(bf16)
    asked = jnp.pad(asked, ((0, 7), (0, 4 * HEAD_DIM - 2 * pairs)))
    weight = jnp.concatenate([wide, narrow], axis=2)
    weight = jnp.concatenate([weight, jnp.broadcast_to(asked, (2,) + asked.shape)], axis=1)
    weight = gather_plane(weight)
    asked = weight[:, :, depth, : 2 * pairs].astype(i32)
    weight = weight[:, :, :depth].reshape(plane * depth, 4 * HEAD_DIM)
    weight = lax.all_gather(weight, "z", axis=0, tiled=True)

    owner, place = asked[:, :, :pairs], asked[:, :, pairs:]
    owner_z, owner_y, owner_c = owner // plane, owner // cores % lines, owner % cores
    wanted = (owner_z * cores + owner_c) * stored + place
    wanted = jnp.take(wanted, other_y(), axis=0, mode="clip").reshape(-1)
    block = jax.ShapeDtypeStruct((cores * pairs, passage_rows, part), bf16)
    outgoing = pl.pallas_call(
        pick_kernel,
        out_shape=[block] * lines,
        in_specs=[SMEM, VMEM],
        out_specs=[VMEM] * lines,
        compiler_params=options,
        name="pick",
    )(wanted, library)
    arrived = [outgoing[0]] + [partner(outgoing[k], "y", k) for k in range(1, lines)]

    here = lax.axis_index("y")
    source = lax.dynamic_index_in_dim(owner_y, here, axis=0, keepdims=False) ^ here
    stored_at = lax.dynamic_index_in_dim(owner * stored + place, here, axis=0, keepdims=False)
    counts = jnp.take(passage_length, stored_at.reshape(-1), axis=0, mode="clip")
    gain, _ = halves(norm_gain[None], part)
    packed = pl.pallas_call(
        pack_kernel,
        out_shape=jax.ShapeDtypeStruct((cores, rows, part), bf16),
        in_specs=[SMEM] * 2 + [VMEM] * (lines + 2),
        out_specs=VMEM,
        compiler_params=options,
        name="pack",
    )(source.reshape(-1), counts, *arrived, queries, gain)

    far = partner(packed, "h", 1)
    own_full = lax.all_gather(packed, "x", axis=0)
    far, own_full = lax.optimization_barrier((far, own_full))
    far = pl.pallas_call(
        spread_kernel,
        out_shape=jax.ShapeDtypeStruct((SIZE["x"],) + packed.shape, bf16),
        in_specs=[VMEM],
        out_specs=VMEM,
        compiler_params=options,
        cost_estimate=pl.CostEstimate(flops=0, bytes_accessed=4 * MIB, transcendentals=0),
        name="spread",
    )(far)
    far_full = lax.all_to_all(far, "x", split_axis=0, concat_axis=0, tiled=True)
    own_swap = partner(own_full, "c", 1)
    far_swap = partner(far_full, "c", 1)

    row = np.arange(rows)
    slot = np.where(row < query_len, row, query_len + (row - query_len) % passage_rows)
    half = HEAD_DIM // 2
    frequency = np.power(10000.0, -2.0 * np.arange(half) / HEAD_DIM).astype(np.float32)
    angles = slot.astype(np.float32)[:, None] * frequency[None, :]
    cosine, sine = np.cos(angles), np.sin(angles)
    attended, own_out = pl.pallas_call(
        functools.partial(attention_kernel, query_len=query_len, passage_rows=passage_rows),
        out_shape=[
            jax.ShapeDtypeStruct((cores, rows, HEAD_DIM), bf16),
            jax.ShapeDtypeStruct((weight.shape[0], HEAD_DIM), bf16),
        ],
        in_specs=[SMEM] + [VMEM] * 7,
        out_specs=[VMEM] * 2,
        scratch_shapes=[pltpu.VMEM((cores * rows, tensors * features), bf16)],
        compiler_params=pltpu.CompilerParams(vmem_limit_bytes=18 * MIB),
        cost_estimate=pl.CostEstimate(
            flops=2 * rows * tensors * features * 6 * HEAD_DIM,
            bytes_accessed=8 * 1024 * 1024,
            transcendentals=2 * rows * rows,
        ),
        name="attention",
    )(
        counts,
        own_full,
        far_full,
        own_swap,
        far_swap,
        weight,
        jnp.asarray(np.concatenate([cosine, cosine], axis=1), f32),
        jnp.asarray(np.concatenate([-sine, sine], axis=1), f32),
    )

    heads = pl.pallas_call(
        heads_kernel,
        out_shape=jax.ShapeDtypeStruct((cores * SIZE["x"], SIZE["h"], rows, HEAD_DIM), bf16),
        in_specs=[VMEM] * 2,
        out_specs=VMEM,
        compiler_params=options,
        name="heads",
    )(attended, partner(attended, "h", 1))
    heads = lax.all_to_all(heads, ("c", "x"), split_axis=0, concat_axis=0, tiled=True)
    core = lax.axis_index("c")
    near_rows = lax.dynamic_index_in_dim(packed, core, axis=0, keepdims=False)
    far_rows = lax.dynamic_slice(
        own_swap, (lax.axis_index("x"), core, 0, 0), (1, 1, rows, part)
    ).reshape(rows, part)
    other_out = partner(own_out, "c", 1)
    return pl.pallas_call(
        functools.partial(
            output_kernel, query_len=query_len, pairs=pairs, passage_rows=passage_rows
        ),
        out_shape=jax.ShapeDtypeStruct((pairs * (query_len + passage_rows), features), bf16),
        in_specs=[VMEM] * 5,
        out_specs=VMEM,
        compiler_params=options,
        cost_estimate=pl.CostEstimate(
            flops=2 * rows * tensors * 2 * HEAD_DIM * features,
            bytes_accessed=3 * 1024 * 1024,
            transcendentals=0,
        ),
        name="output",
    )(heads, own_out, other_out, near_rows, far_rows)


def solution(mesh):
    fine = Mesh(mesh.devices.reshape([size for _, size in SPLIT]), AXES)
    placed = (
        P(CORPUS, None, TENSOR),
        P(CORPUS, None, TENSOR),
        P(),
        P(CORPUS, None),
        P(CORPUS, None),
        P(TENSOR),
        P(CORPUS, None, TENSOR),
        P(TENSOR, CORPUS),
    )
    return jax.shard_map(
        on_device, mesh=fine, in_specs=placed, out_specs=P(CORPUS, TENSOR), check_vma=False
    )
```
